256 devices in a mesh: dp: 64 (over z, y, core), group: 4 (over x).
Axes of the slice: x: 4, y: 4, z: 8, core: 2. Of those that a mesh axis runs over, the one named last changes fastest.
Arguments:
- cotangent: bfloat16 [32768, 512], P('dp', 'group'), may hold values from -6 to 6
- saved_inputs: bfloat16 [3, 32768, 512], P(None, 'dp'), may hold values from -6 to 6
- weights: bfloat16 [3, 512, 512], replicated, may hold values from -0.25 to 0.25
- edge_values: bfloat16 [8192, 128, 128], P('dp'), may hold values from -0.25 to 0.25
- edge_rows: int32 [8192], P('dp'), may hold values from 0 to 3
- edge_cols: int32 [8192], P('dp'), may hold values from 0 to 255, as said below
- edge_counts: int32 [64], P('dp'), may hold values from 96 to 128, as said below
- block_owner: int32 [256], replicated, may hold values from 0 to 255, as said below
Outputs:
- input_grad: bfloat16 [32768, 512], P('dp', 'group')
- weight_grad: float32 [3, 512, 512], P(None, None, 'group')
The draws below stay inside these ranges and needn't reach their ends.
Inputs may be any that keep to these rules, and one draw needn't show every extreme that they name: `edge_cols`: column block ids; among the live edge slots of one dp index, those whose blocks are stored on any one dp index reach at most 2 different column blocks, and some dp index is reached with 2 blocks by the live edges of every dp index. `edge_counts`: number of live slots at the head of each dp index's edge slots; the others are empty. Some dp index has all of its slots live. `block_owner`: each storage position appears once.
All inputs are finite; a program needn't handle non-finite values.
Results may differ from the reference program's by a relative error of at most 0.03.
Values may be sent and summed in bfloat16 or wider, within the bound.
No kernel may reach another device: no remote copies, remote signals or barrier semaphores. Data moves between devices by JAX's collectives and lax.ppermute only.
A program may use at most 128 MiB of HBM per device.

```python
import math
import jax
import jax.numpy as jnp
from jax import lax

D = 512
BLK = 128
NB_DEV = 4
HOPS = 3
CAP = 2
EDGE_REP = 2
PEERS = 32
EDGE_DEV = 128
NBLOCKS = 256
NODES = 32768
EDGES = 8192
N_DP = 64


def layout(key):
    owner_key, score_key, k_heavy, k_hub, first_key, k_step, k_order = jax.random.split(key, 7)
    owner = jax.random.permutation(owner_key, NBLOCKS).astype(jnp.int32)
    hub_dev = jax.random.randint(k_hub, (), 0, N_DP)
    heavy_blocks = jax.random.randint(k_heavy, (4,), 0, N_DP)
    device_list = jnp.arange(N_DP, dtype=jnp.int32)
    extra_credit = jnp.sum((device_list[None, :] == heavy_blocks[:, None]).astype(jnp.int32), axis=0) * 2 ** 12
    block_scores = jax.random.randint(score_key, (N_DP, N_DP), 0, 2 ** 12) + extra_credit[None, :]
    block_scores = block_scores + (device_list == hub_dev).astype(jnp.int32)[None, :] * 2 ** 16
    block_scores = block_scores * N_DP + device_list[None, :]
    chosen = jnp.argsort(-block_scores, axis=1)[:, :PEERS].astype(jnp.int32)
    first = jax.random.randint(first_key, (N_DP, PEERS), 0, NB_DEV)
    stride = jax.random.randint(k_step, (N_DP, PEERS), 1, NB_DEV // CAP + 1)
    locs = (first[:, :, None] + jnp.arange(CAP, dtype=jnp.int32)[None, None, :] * stride[:, :, None]) % NB_DEV
    slot_position = chosen[:, :, None] * NB_DEV + locs
    slot_position = jnp.repeat(slot_position, EDGE_REP, axis=2).reshape(N_DP, EDGE_DEV)
    head = CAP * EDGE_REP
    order_keys = jax.random.split(k_order, N_DP)
    tails = jax.vmap(lambda sub: jax.random.permutation(sub, EDGE_DEV - head))(order_keys).astype(jnp.int32)
    order = jnp.concatenate([jnp.broadcast_to(jnp.arange(head, dtype=jnp.int32), (N_DP, head)), head + tails], axis=1)
    slot_position = jnp.take_along_axis(slot_position, order, axis=1)
    inverse = jnp.zeros((NBLOCKS,), jnp.int32).at[owner].set(jnp.arange(NBLOCKS, dtype=jnp.int32))
    return (owner, inverse[slot_position].reshape(-1))


def draw_edge_cols(key, part):
    return layout(key)[1]


def draw_block_owner(key, part):
    return layout(key)[0]


def draw_edge_counts(key, part):
    key = jax.random.fold_in(key, 7)
    k_count, k_full = jax.random.split(key)
    counts = jax.random.randint(k_count, (N_DP,), 3 * EDGE_DEV // 4, EDGE_DEV + 1)
    full_dev = jax.random.randint(k_full, (), 0, N_DP)
    return counts.at[full_dev].set(EDGE_DEV).astype(jnp.int32)


def place_ends(values, stream_key, low, top_value):
    place = [jax.random.randint(jax.random.fold_in(stream_key, axis), (), 0, length) for axis, length in enumerate(values.shape)]
    longest = values.shape.index(max(values.shape))
    neighbour = place[:longest] + [(place[longest] + 1) % values.shape[longest]] + place[longest + 1:]
    return values.at[tuple(place)].set(low).at[tuple(neighbour)].set(top_value)


def level_of(key, dims, cuts, smallest, largest):
    def one(axis_at, parts):
        draws = jax.random.uniform(jax.random.fold_in(jax.random.fold_in(key, 6), axis_at), (parts,), jnp.float32, smallest / len(cuts), largest / len(cuts))
        return jnp.repeat(jnp.exp(draws), dims[axis_at] // parts).reshape((-1,) + (1,) * (len(dims) - axis_at - 1))

    factor_of = one(*cuts[0])
    for cut in cuts[1:]:
        factor_of = factor_of * one(*cut)
    return factor_of


def gaussian(rng, extent, width, bound, shards=(), kind=jnp.bfloat16):
    level = level_of(rng, extent, shards, -0.22, 0.18) if shards else 1.0
    values = jax.random.normal(rng, extent, jnp.float32) * width * level
    return jnp.minimum(jnp.maximum(values, -bound), bound).astype(kind)


def setup_inputs(seed: int = 0) -> dict:
    keys = jax.random.split(jax.random.key(seed), 9)
    cotangent = gaussian(keys[0], (NODES, D), 1.0, 6.0, ((0, 64), (1, 4)))
    saved_inputs = gaussian(keys[1], (HOPS, NODES, D), 1.0, 6.0, ((1, 64),))
    weights = gaussian(keys[2], (HOPS, D, D), D ** -0.5, 0.25)
    edge_values = gaussian(keys[3], (EDGES, BLK, BLK), (BLK * 4) ** -0.5, 0.25, ((0, 64),))
    edge_rows = place_ends(jax.random.randint(keys[4], (EDGES,), 0, NB_DEV), jax.random.fold_in(keys[4], 1), 0, NB_DEV - 1).astype(jnp.int32)
    edge_cols = draw_edge_cols(jax.random.fold_in(keys[8], 71), 0)
    edge_counts = draw_edge_counts(jax.random.fold_in(keys[8], 71), 0)
    block_owner = draw_block_owner(jax.random.fold_in(keys[8], 71), 0)
    return dict(cotangent=cotangent, saved_inputs=saved_inputs, weights=weights, edge_values=edge_values, edge_rows=edge_rows, edge_cols=edge_cols, edge_counts=edge_counts, block_owner=block_owner)


def silu_slope(value):
    sigma = jax.nn.sigmoid(value)
    return sigma * (1.0 + value * (1.0 - sigma))

def routing(column_ids, edge_count, block_owner, peers, blocks_dev):
    edge_total = column_ids.shape[0]
    live_mask = jnp.arange(edge_total, dtype=jnp.int32) < edge_count
    slot_position = block_owner[column_ids].astype(jnp.int32)
    owner_dev = slot_position // blocks_dev
    local_block = slot_position % blocks_dev
    all_cells = jnp.arange(peers * blocks_dev, dtype=jnp.int32)
    present = jnp.any((slot_position[:, None] == all_cells[None, :]) & live_mask[:, None], axis=0)
    present = present.reshape(peers, blocks_dev).astype(jnp.int32)
    ranking = jnp.cumsum(present, axis=1) - present
    slot_ids = owner_dev * CAP + ranking.reshape(-1)[slot_position]
    block_range = jnp.arange(blocks_dev, dtype=jnp.int32)
    targets = jnp.stack([lax.optimization_barrier(jnp.sum(block_range[None, :] * present * (ranking == slot_index).astype(jnp.int32), axis=1)) for slot_index in range(CAP)], axis=1)
    return (live_mask, slot_ids.astype(jnp.int32), targets.astype(jnp.int32))

def reference(cotangent, saved_inputs, weights, edge_values, edge_rows, edge_cols, edge_counts, block_owner):
    grad = cotangent.astype(jnp.float32)
    values_dev = edge_values.reshape(N_DP, EDGE_DEV, BLK, BLK)
    rows_dev = edge_rows.reshape(N_DP, EDGE_DEV)
    cols_dev = edge_cols.reshape(N_DP, EDGE_DEV)
    scale = 1.0 / math.sqrt(NODES)
    weight_list = []
    for layer_index in reversed(range(HOPS)):
        inputs_hop = saved_inputs[layer_index]
        weight_hop = weights[layer_index]
        preact = jnp.dot(inputs_hop, weight_hop, preferred_element_type=jnp.float32)
        slopes = (grad * silu_slope(preact)).astype(jnp.bfloat16)
        weight_list.append(jnp.dot(inputs_hop.T, slopes, preferred_element_type=jnp.float32) * scale)
        upstream = jnp.dot(slopes, weight_hop.T, preferred_element_type=jnp.float32).astype(jnp.bfloat16)
        upstream = upstream.reshape(N_DP, NB_DEV, BLK, D)

        def one_source(running, packed):
            block_vals, row_ids, column_ids, edge_count, upstream_dev = packed
            live_mask, slot_ids, targets = routing(column_ids, edge_count, block_owner, N_DP, NB_DEV)
            gathered_rows = upstream_dev[row_ids].astype(jnp.float32)
            contrib = jnp.einsum('eij,eif->ejf', block_vals.astype(jnp.float32), gathered_rows)
            contrib = jnp.where(live_mask[:, None, None], contrib, 0.0)
            messages = jax.ops.segment_sum(contrib, slot_ids, num_segments=N_DP * CAP).astype(jnp.bfloat16)
            destinations = (jnp.arange(N_DP, dtype=jnp.int32)[:, None] * NB_DEV + targets).reshape(-1)
            running = running.at[destinations].add(messages.astype(jnp.float32))
            return (running, None)
        start_total = jnp.zeros((NBLOCKS, BLK, D), jnp.float32)
        arrived, unused = lax.scan(one_source, start_total, (values_dev, rows_dev, cols_dev, edge_counts, upstream))
        grad = grad + arrived.reshape(NODES, D)
    weight_grad = jnp.stack(weight_list[::-1], axis=0)
    return (grad.astype(jnp.bfloat16), weight_grad)
```

```python
import math

import jax
import jax.numpy as jnp
from jax import lax
from jax.experimental import pallas as pl
from jax.experimental.pallas import tpu as pltpu
from jax.sharding import PartitionSpec as P

BLK = 128
HOPS = 3
NZ, NY, NC = 8, 4, 2
NX = 4
NB = 4
SLOTS = NZ * NY * NB
EDGES = 256
UNROLL = 8
ITEMS = 200
HALF = 64

bf16 = jnp.bfloat16
f32 = jnp.float32
MB = 1 << 20


def index_of(z, y, c):
    return ((z % NZ) * NY + (y % NY)) * NC + c


def shift(dz=0, dy=0, dc=0):
    return [
        (index_of(z, y, c), index_of(z + dz, y + dy, c ^ dc))
        for z in range(NZ)
        for y in range(NY)
        for c in range(NC)
    ]


Y_GROUPS = [[index_of(z, y, c) for y in range(NY)] for z in range(NZ) for c in range(NC)]
Z_GROUPS = [[index_of(z, y, c) for z in range(NZ)] for y in range(NY) for c in range(NC)]


YZ_GROUPS = [[index_of(z, y, c) for z in range(NZ) for y in range(NY)] for c in range(NC)]
PAIR = (2, NY // 2, NB, HALF, BLK)
SUM_Y_COST = 1
WTIE = 2
STIE = 4


def cost(us):
    return pl.CostEstimate(flops=0, bytes_accessed=int(us * 3_300_000), transcendentals=0)


def silu_slope(value):
    sigma = jax.nn.sigmoid(value)
    return sigma * (1.0 + value * (1.0 - sigma))


def vmem():
    return pl.BlockSpec(memory_space=pltpu.VMEM)


def params(limit):
    return pltpu.CompilerParams(vmem_limit_bytes=limit)


def factor_kernel(member, x_ref, w_ref, d_ref):
    for r in range(NB):
        z = jnp.dot(x_ref[0, r * BLK : (r + 1) * BLK, :], w_ref[0], preferred_element_type=f32)
        d_ref[r] = silu_slope(z.T)


def factors(member, saved, weights, hop):
    return pl.pallas_call(
        factor_kernel,
        out_shape=jax.ShapeDtypeStruct((NB, BLK, BLK), f32),
        grid_spec=pltpu.PrefetchScalarGridSpec(
            num_scalar_prefetch=1,
            grid=(1,),
            in_specs=[
                pl.BlockSpec((1, 512, 512), lambda i, m: (hop, 0, 0)),
                pl.BlockSpec((1, 512, BLK), lambda i, m: (hop, 0, m[0])),
            ],
            out_specs=pl.BlockSpec((NB, BLK, BLK), lambda i, m: (0, 0, 0)),
        ),
        compiler_params=params(16 * MB),
        name="factors",
    )(member, saved, weights)


def first_kernel(member, x_ref, w_ref, cot_ref, grad_ref, slope_ref):
    for r in range(NB):
        rows = slice(r * BLK, (r + 1) * BLK)
        z = jnp.dot(x_ref[0, rows, :], w_ref[0], preferred_element_type=f32)
        grad = cot_ref[rows, :].astype(f32).T
        grad_ref[r] = grad
        slope_ref[r] = (grad * silu_slope(z.T)).astype(bf16)


def first_slopes(member, saved, weights, cotangent):
    hop = HOPS - 1
    whole = pl.BlockSpec((NB, BLK, BLK), lambda i, m: (0, 0, 0))
    return pl.pallas_call(
        first_kernel,
        out_shape=(
            jax.ShapeDtypeStruct((NB, BLK, BLK), f32),
            jax.ShapeDtypeStruct((NB, BLK, BLK), bf16),
        ),
        grid_spec=pltpu.PrefetchScalarGridSpec(
            num_scalar_prefetch=1,
            grid=(1,),
            in_specs=[
                pl.BlockSpec((1, 512, 512), lambda i, m: (hop, 0, 0)),
                pl.BlockSpec((1, 512, BLK), lambda i, m: (hop, 0, m[0])),
                pl.BlockSpec((512, BLK), lambda i, m: (0, 0)),
            ],
            out_specs=(whole, whole),
        ),
        compiler_params=params(16 * MB),
        name="first_slopes",
    )(member, saved, weights, cotangent)


def upstream_kernel(member, w_ref, s0, s1, s2, s3, u_ref):
    me = member[0]
    parts = []
    for d in range(NX):
        start = pl.multiple_of(lax.rem(me - d + NX, NX) * BLK, BLK)
        parts.append(w_ref[0, :, pl.ds(start, BLK)])
    lhs = jnp.concatenate(parts, axis=1)
    for r in range(NB):
        rhs = jnp.concatenate([s[r] for s in (s0, s1, s2, s3)], axis=0)
        u_ref[r] = jnp.dot(lhs, rhs, preferred_element_type=f32).astype(bf16)


def upstream_of(member, weights, hop, pieces):
    whole = pl.BlockSpec((NB, BLK, BLK), lambda i, m: (0, 0, 0))
    return pl.pallas_call(
        upstream_kernel,
        out_shape=jax.ShapeDtypeStruct((NB, BLK, BLK), bf16),
        grid_spec=pltpu.PrefetchScalarGridSpec(
            num_scalar_prefetch=1,
            grid=(1,),
            in_specs=[pl.BlockSpec((1, BLK, 512), lambda i, m: (hop, m[0], 0))] + [whole] * NX,
            out_specs=whole,
        ),
        compiler_params=params(16 * MB),
        name="upstream",
    )(member, weights, *pieces)


def weight_kernel(x_ref, s0, s1, s2, out_ref, *, scale):
    for hop, s_ref in enumerate((s0, s1, s2)):
        lhs = jnp.concatenate([s_ref[r] for r in range(NB)], axis=1)
        part = jnp.dot(lhs, x_ref[hop], preferred_element_type=f32)
        out_ref[hop * 512 : (hop + 1) * 512, :] = part.T * scale


def weight_parts(saved, slopes, scale):
    whole = pl.BlockSpec((NB, BLK, BLK), lambda i: (0, 0, 0))
    return pl.pallas_call(
        lambda *refs: weight_kernel(*refs, scale=scale),
        out_shape=jax.ShapeDtypeStruct((HOPS * 512, BLK), f32),
        grid=(1,),
        in_specs=[pl.BlockSpec((HOPS, 512, 512), lambda i: (0, 0, 0))] + [whole] * HOPS,
        out_specs=pl.BlockSpec((HOPS * 512, BLK), lambda i: (0, 0)),
        compiler_params=params(16 * MB),
        cost_estimate=cost(3),
        name="weight_parts",
    )(saved, *slopes)


def total_kernel(x_ref, out_ref):
    total = x_ref[0]
    for i in range(1, x_ref.shape[0]):
        total += x_ref[i]
    out_ref[...] = total


def total_of(x):
    return pl.pallas_call(
        total_kernel,
        out_shape=jax.ShapeDtypeStruct(x.shape[1:], f32),
        in_specs=[vmem()],
        out_specs=vmem(),
        compiler_params=params(8 * MB),
        cost_estimate=cost(1),
        name="total",
    )(x)


def spread_kernel(a_ref, b_ref, out_ref):
    total = a_ref[...] + b_ref[...]
    for i in range(NZ * NY):
        out_ref[i] = total


def spread(a, b):
    return pl.pallas_call(
        spread_kernel,
        out_shape=jax.ShapeDtypeStruct((NZ * NY,) + a.shape, f32),
        grid=(1,),
        in_specs=[pl.BlockSpec(a.shape, lambda i: (0, 0))] * 2,
        out_specs=pl.BlockSpec((NZ * NY,) + a.shape, lambda i: (0, 0, 0)),
        compiler_params=params(8 * MB),
        cost_estimate=cost(1),
        name="spread",
    )(a, b)


def message_kernel(table, own_ref, sib_ref, a_own, a_sib, out_a, *rest):
    out_b = rest[:NZ]
    edges, acc, up, stage, stage_b, sems, out_sems, out_b_sems = rest[NZ:]
    copies = [
        pltpu.make_async_copy(a_own, edges.at[pl.ds(0, EDGES // 2)], sems.at[0]),
        pltpu.make_async_copy(a_sib, edges.at[pl.ds(EDGES // 2, EDGES // 2)], sems.at[1]),
    ]
    for copy in copies:
        copy.start()
    up[0:NB] = own_ref[...]
    up[NB : 2 * NB] = sib_ref[...]
    up[2 * NB] = jnp.zeros((BLK, BLK), bf16)

    @pl.loop(0, SLOTS // 4)
    def _(i):
        acc[pl.ds(i * 4, 4)] = jnp.zeros((4, BLK, BLK), f32)

    for copy in copies:
        copy.wait()

    n_items = table[5 * ITEMS]

    @pl.loop(0, (n_items + UNROLL - 1) // UNROLL)
    def _(i):
        sums = []
        for j in range(UNROLL):
            at = i * UNROLL + j
            lhs = jnp.concatenate([up[table[3 * ITEMS + at]], up[table[4 * ITEMS + at]]], axis=1)
            rhs = jnp.concatenate([edges[table[ITEMS + at]], edges[table[2 * ITEMS + at]]], axis=0)
            sums.append(jnp.dot(lhs, rhs, preferred_element_type=f32))
        for j in range(UNROLL):
            slot = table[i * UNROLL + j]
            acc[slot] = acc[slot] + sums[j]

    z, y = table[5 * ITEMS + 1], table[5 * ITEMS + 2]
    sends = []
    for dz in range(NZ):
        for dy in range(NY):
            place = dz * 2 + dy // 2
            for b in range(NB):
                total = acc[(dz * NY + dy) * NB + b].astype(bf16)
                stage[dz, dy, b] = total[:HALF]
                stage_b[(place + 1) // 2 % NZ, (place + 1) % 2, dy % 2, b] = total[HALF:]
            send = pltpu.make_async_copy(
                stage.at[dz, dy],
                out_a.at[lax.rem(y + dy, NY), lax.rem(z + dz, NZ)],
                out_sems.at[dz * NY + dy],
            )
            send.start()
            sends.append(send)
        ready = [dz] if dz else []
        if dz == NZ - 1:
            ready.append(0)
        for pair in ready:
            send = pltpu.make_async_copy(stage_b.at[pair], out_b[pair], out_b_sems.at[pair])
            send.start()
            sends.append(send)
    for send in sends:
        send.wait()


def messages_of(table, own, sibling, a_own, a_sib):
    hbm = pl.BlockSpec(memory_space=pltpu.HBM)
    return pl.pallas_call(
        message_kernel,
        out_shape=(jax.ShapeDtypeStruct((NY, NZ, NB, HALF, BLK), bf16),)
        + (jax.ShapeDtypeStruct(PAIR, bf16),) * NZ,
        in_specs=[pl.BlockSpec(memory_space=pltpu.SMEM), vmem(), vmem(), hbm, hbm],
        out_specs=(hbm,) * (NZ + 1),
        scratch_shapes=[
            pltpu.VMEM((EDGES, BLK, BLK), bf16),
            pltpu.VMEM((SLOTS + 1, BLK, BLK), f32),
            pltpu.VMEM((2 * NB + 1, BLK, BLK), bf16),
            pltpu.VMEM((NZ, NY, NB, HALF, BLK), bf16),
            pltpu.VMEM((NZ,) + PAIR, bf16),
            pltpu.SemaphoreType.DMA((2,)),
            pltpu.SemaphoreType.DMA((NZ * NY,)),
            pltpu.SemaphoreType.DMA((NZ,)),
        ],
        compiler_params=params(60 * MB),
        cost_estimate=cost(6),
        name="messages",
    )(table, own, sibling, a_own, a_sib)


def arrivals(from_z, from_y, r):
    first = from_z[0, r].astype(f32)
    for i in range(1, NZ):
        first += from_z[i, r].astype(f32)
    second = from_y[0][r].astype(f32)
    for part in from_y[1:]:
        second += part[r].astype(f32)
    return jnp.concatenate([first, second], axis=0)


def update_kernel(from_z, *refs):
    from_y, (grad_ref, d_ref, new_ref, slope_ref) = refs[:NY], refs[NY:]
    for r in range(NB):
        grad = grad_ref[r] + arrivals(from_z, from_y, r)
        new_ref[r] = grad
        slope_ref[r] = (grad * d_ref[r]).astype(bf16)


def update(from_z, from_y, grad, factor):
    return pl.pallas_call(
        update_kernel,
        out_shape=(
            jax.ShapeDtypeStruct((NB, BLK, BLK), f32),
            jax.ShapeDtypeStruct((NB, BLK, BLK), bf16),
        ),
        in_specs=[vmem()] * (NY + 3),
        out_specs=(vmem(), vmem()),
        compiler_params=params(16 * MB),
        cost_estimate=cost(1),
        name="update",
    )(from_z, *from_y, grad, factor)


def last_kernel(from_z, *refs):
    from_y, (grad_ref, out_ref) = refs[:NY], refs[NY:]
    for r in range(NB):
        grad = grad_ref[r] + arrivals(from_z, from_y, r)
        out_ref[r * BLK : (r + 1) * BLK, :] = grad.T.astype(bf16)


def last_update(from_z, from_y, grad):
    return pl.pallas_call(
        last_kernel,
        out_shape=jax.ShapeDtypeStruct((NB * BLK, BLK), bf16),
        in_specs=[vmem()] * (NY + 2),
        out_specs=vmem(),
        compiler_params=params(16 * MB),
        cost_estimate=cost(1),
        name="last_update",
    )(from_z, *from_y, grad)


def plus(a, b):
    return (a.astype(f32) + b.astype(f32)).astype(bf16)


def fetch(held, sems, *sources):
    copies = [
        pltpu.make_async_copy(q, held.at[i], sems.at[i]) for i, q in enumerate(sources)
    ]
    for copy in copies:
        copy.start()
    for copy in copies:
        copy.wait()


def step_kernel(q_up, q_down, got_up, got_down, up, down, held, sems):
    fetch(held, sems, q_up, q_down)
    up[...] = plus(held[0], got_up[...])
    down[...] = plus(held[1], got_down[...])


def final_kernel(q_up, q_down, got_up, got_down, up, down, keep, held, sems):
    fetch(held, sems, q_up, q_down)
    up[...] = plus(held[0, 1], got_up[1])
    down[...] = plus(held[1, 0], got_down[0])
    keep[0] = held[1, 1].astype(f32) + got_down[1].astype(f32)
    keep[1] = held[0, 0].astype(f32) + got_up[0].astype(f32)


def step(q_up, q_down, got_up, got_down, final):
    hbm = pl.BlockSpec(memory_space=pltpu.HBM)
    sent = jax.ShapeDtypeStruct(PAIR[1:] if final else PAIR, bf16)
    kept = (jax.ShapeDtypeStruct(PAIR, f32),) if final else ()
    return pl.pallas_call(
        final_kernel if final else step_kernel,
        out_shape=(sent, sent) + kept,
        in_specs=[hbm, hbm, vmem(), vmem()],
        out_specs=(vmem(),) * (3 if final else 2),
        scratch_shapes=[pltpu.VMEM((2,) + PAIR, bf16), pltpu.SemaphoreType.DMA((2,))],
        compiler_params=params(4 * MB),
        cost_estimate=cost(0.5),
        name="final_step" if final else "step",
    )(q_up, q_down, got_up, got_down)


def ring_end_kernel(keep, last_up, last_down, *out):
    for i, last in enumerate((last_up, last_down)):
        total = keep[i] + last[...].astype(f32)
        for j in range(NY // 2):
            at = out[i * (NY // 2) + j]
            at[...] = total[j].astype(at.dtype)


def ring_end(keep, last_up, last_down):
    shape = (NB, HALF, BLK)
    return pl.pallas_call(
        ring_end_kernel,
        out_shape=(jax.ShapeDtypeStruct(shape, f32),)
        + (jax.ShapeDtypeStruct(shape, bf16),) * (NY - 1),
        in_specs=[vmem()] * 3,
        out_specs=(vmem(),) * NY,
        compiler_params=params(4 * MB),
        cost_estimate=cost(0.5),
        name="ring_end",
    )(keep, last_up, last_down)


def ring(q, tie):
    ahead, back = shift(dz=1), shift(dz=-1)
    up, down = q[NZ // 2], q[NZ // 2 + 1]
    keep = None
    for k in range(1, NZ // 2):
        got_up = lax.ppermute(up, "dp", ahead)
        got_down = lax.ppermute(down, "dp", back)
        got_up, got_down = tie(k, got_up, got_down)
        args = (q[NZ // 2 - k], q[(NZ // 2 + 1 + k) % NZ], got_up, got_down)
        up, down, *keep = step(*args, k == NZ // 2 - 1)
    last_up = lax.ppermute(up, "dp", ahead)
    last_down = lax.ppermute(down, "dp", back)
    last_up, last_down = tie(NZ // 2, last_up, last_down)
    return ring_end(*keep, last_up, last_down)


def sum_y_kernel(x_ref, out_ref):
    total = x_ref[0].astype(f32)
    for i in range(1, NY):
        total += x_ref[i].astype(f32)
    out_ref[...] = total.astype(bf16)


def sum_y(x):
    return pl.pallas_call(
        sum_y_kernel,
        out_shape=jax.ShapeDtypeStruct(x.shape[1:], bf16),
        grid=(NZ,),
        in_specs=[pl.BlockSpec((NY, 1, NB, HALF, BLK), lambda i: (0, i, 0, 0, 0))],
        out_specs=pl.BlockSpec((1, NB, HALF, BLK), lambda i: (i, 0, 0, 0)),
        compiler_params=params(8 * MB),
        cost_estimate=cost(SUM_Y_COST),
        name="sum_y",
    )(x)


def exchange(out_a, out_b, parts=None):
    by_y = lax.all_to_all(out_a, "dp", 0, 0, axis_index_groups=Y_GROUPS, tiled=True)
    made = {"sums": sum_y(by_y)}
    if parts is not None:
        made["copies"] = spread_parts(parts)

    def tie(k, up, down):
        if k == STIE:
            up, down, made["sums"] = lax.optimization_barrier((up, down, made["sums"]))
        if parts is not None and k == WTIE:
            up, down, made["copies"] = lax.optimization_barrier((up, down, made["copies"]))
            made["grads"] = collect(made["copies"])
        return up, down

    own, *others = ring(out_b, tie)
    from_z = lax.all_to_all(made["sums"], "dp", 0, 0, axis_index_groups=Z_GROUPS, tiled=True)
    from_y = [own] + [lax.ppermute(x, "dp", shift(dy=d + 1)) for d, x in enumerate(others)]
    return from_z, from_y, made.get("grads")


def routing(edge_rows, edge_cols, edge_counts, block_owner, z, y, c):
    live = jnp.arange(EDGES // 2, dtype=jnp.int32) < edge_counts[0]
    code = jnp.where(live, block_owner[edge_cols], -1)
    mine = jnp.stack([code, edge_rows])
    theirs = lax.ppermute(mine, "dp", shift(dc=1))
    code = jnp.concatenate([mine[0], theirs[0]])
    rows = jnp.concatenate([mine[1], theirs[1] + NB])
    dev = code // NB
    used = (code >= 0) & (dev % NC == c)
    y_to, z_to = (dev // NC) % NY, dev // (NC * NY)
    slot = jnp.where(used, ((z_to - z + NZ) % NZ * NY + (y_to - y + NY) % NY) * NB + code % NB, SLOTS)
    ids = jnp.arange(EDGES, dtype=jnp.int32)
    slots = jnp.arange(SLOTS, dtype=jnp.int32)
    same = (slot[:, None] == slot[None, :]) & (ids[None, :] < ids[:, None])
    rank = jnp.sum(same.astype(jnp.int32), axis=1)
    hit = (slot[:, None] == slots[None, :]).astype(jnp.int32)
    pairs = (jnp.sum(hit, axis=0) + 1) // 2
    base = jnp.sum(jnp.where(slots[None, :] < slots[:, None], pairs[None, :], 0), axis=1)
    item = jnp.where(used, jnp.sum(hit * base[None, :], axis=1) + rank // 2, -1)
    side = rank % 2
    place = jnp.arange(ITEMS, dtype=jnp.int32)
    at = [
        (place[:, None] == item[None, :]) & (side[None, :] == s) for s in range(2)
    ]

    def pick(mask, values, default):
        return jnp.sum(jnp.where(mask, values[None, :] - default, 0), axis=1) + default

    return jnp.concatenate(
        [
            pick(at[0], slot, SLOTS),
            pick(at[0], ids, 0),
            pick(at[1], ids, 0),
            pick(at[0], rows, 2 * NB),
            pick(at[1], rows, 2 * NB),
            jnp.stack([jnp.sum(pairs), z, y]),
        ]
    ).astype(jnp.int32)


def spread_parts(parts):
    rows = parts.shape[0] // (NZ * NY)
    got = lax.all_to_all(parts, "dp", 0, 0, axis_index_groups=YZ_GROUPS, tiled=True)
    mine = total_of(got.reshape(NZ * NY, rows, BLK))
    return spread(mine, lax.ppermute(mine, "dp", shift(dc=1)))


def collect(copies):
    whole = lax.all_to_all(copies, "dp", 0, 0, axis_index_groups=YZ_GROUPS, tiled=True)
    return whole.reshape(HOPS, 512, BLK)


def on_device(
    cotangent, saved_inputs, weights, edge_values, edge_rows, edge_cols, edge_counts, block_owner
):
    scale = 1.0 / math.sqrt(saved_inputs.shape[1] * lax.axis_size("dp"))
    dp = lax.axis_index("dp")
    z, y, c = dp // (NY * NC), dp // NC % NY, dp % NC
    group = lax.axis_index("group")
    member = jnp.full((1,), group, jnp.int32)

    edges_sib = lax.ppermute(edge_values, "dp", shift(dc=1))
    table = routing(edge_rows, edge_cols, edge_counts, block_owner, z, y, c)
    grad, slopes = first_slopes(member, saved_inputs, weights, cotangent)
    factor = [factors(member, saved_inputs, weights, h) for h in range(HOPS - 1)]

    kept = [None] * HOPS
    for hop in reversed(range(HOPS)):
        kept[hop] = slopes
        pieces = [slopes] + [
            lax.ppermute(slopes, "group", [(i, (i + d) % NX) for i in range(NX)])
            for d in range(1, NX)
        ]
        own = upstream_of(member, weights, hop, pieces)
        sibling = lax.ppermute(own, "dp", shift(dc=1))
        out_a, *out_b = messages_of(table, own, sibling, edge_values, edges_sib)
        if hop:
            from_z, from_y, _ = exchange(out_a, out_b)
            grad, slopes = update(from_z, from_y, grad, factor[hop - 1])
        else:
            parts = weight_parts(saved_inputs, kept, scale)
            from_z, from_y, weight_grad = exchange(out_a, out_b, parts)
            result = last_update(from_z, from_y, grad)
    return result, weight_grad


def solution(mesh):
    in_specs = (
        P("dp", "group"),
        P(None, "dp", None),
        P(),
        P("dp", None, None),
        P("dp"),
        P("dp"),
        P("dp"),
        P(),
    )
    out_specs = (P("dp", "group"), P(None, None, "group"))
    return jax.shard_map(
        on_device, mesh=mesh, in_specs=in_specs, out_specs=out_specs, check_vma=False
    )
```

```python
import math

import jax
import jax.numpy as jnp
from jax import lax
from jax.experimental import pallas as pl
from jax.experimental.pallas import tpu as pltpu
from jax.sharding import PartitionSpec as P

BLK = 128
HOPS = 3
NZ, NY, NC = 8, 4, 2
NX = 4
NB = 4
SLOTS = NZ * NY * NB
EDGES = 256
UNROLL = 8
ITEMS = 264
HALF = 64

bf16 = jnp.bfloat16
f32 = jnp.float32
MB = 1 << 20


def index_of(z, y, c):
    return ((z % NZ) * NY + (y % NY)) * NC + c


def shift(dz=0, dy=0, dc=0):
    return [
        (index_of(z, y, c), index_of(z + dz, y + dy, c ^ dc))
        for z in range(NZ)
        for y in range(NY)
        for c in range(NC)
    ]


Y_GROUPS = [[index_of(z, y, c) for y in range(NY)] for z in range(NZ) for c in range(NC)]
Z_GROUPS = [[index_of(z, y, c) for z in range(NZ)] for y in range(NY) for c in range(NC)]


YZ_GROUPS = [[index_of(z, y, c) for z in range(NZ) for y in range(NY)] for c in range(NC)]
PAIR = (2, NY // 2, NB, HALF, BLK)
SUM_Y_COST = 1
STIE = 4


def cost(us):
    return pl.CostEstimate(flops=0, bytes_accessed=int(us * 3_300_000), transcendentals=0)


def silu_slope(value):
    sigma = jax.nn.sigmoid(value)
    return sigma * (1.0 + value * (1.0 - sigma))


def vmem():
    return pl.BlockSpec(memory_space=pltpu.VMEM)


def params(limit):
    return pltpu.CompilerParams(vmem_limit_bytes=limit)


def factor_kernel(member, x_ref, w_ref, d_ref):
    for r in range(NB):
        z = jnp.dot(x_ref[0, r * BLK : (r + 1) * BLK, :], w_ref[0], preferred_element_type=f32)
        d_ref[r] = silu_slope(z.T)


def factors(member, saved, weights, hop):
    return pl.pallas_call(
        factor_kernel,
        out_shape=jax.ShapeDtypeStruct((NB, BLK, BLK), f32),
        grid_spec=pltpu.PrefetchScalarGridSpec(
            num_scalar_prefetch=1,
            grid=(1,),
            in_specs=[
                pl.BlockSpec((1, 512, 512), lambda i, m: (hop, 0, 0)),
                pl.BlockSpec((1, 512, BLK), lambda i, m: (hop, 0, m[0])),
            ],
            out_specs=pl.BlockSpec((NB, BLK, BLK), lambda i, m: (0, 0, 0)),
        ),
        compiler_params=params(60 * MB),
        name="factors",
    )(member, saved, weights)


def first_kernel(member, x_ref, w_ref, cot_ref, grad_ref, slope_ref):
    for r in range(NB):
        rows = slice(r * BLK, (r + 1) * BLK)
        z = jnp.dot(x_ref[0, rows, :], w_ref[0], preferred_element_type=f32)
        grad = cot_ref[rows, :].astype(f32).T
        grad_ref[r] = grad
        slope_ref[r] = (grad * silu_slope(z.T)).astype(bf16)


def first_slopes(member, saved, weights, cotangent):
    hop = HOPS - 1
    whole = pl.BlockSpec((NB, BLK, BLK), lambda i, m: (0, 0, 0))
    return pl.pallas_call(
        first_kernel,
        out_shape=(
            jax.ShapeDtypeStruct((NB, BLK, BLK), f32),
            jax.ShapeDtypeStruct((NB, BLK, BLK), bf16),
        ),
        grid_spec=pltpu.PrefetchScalarGridSpec(
            num_scalar_prefetch=1,
            grid=(1,),
            in_specs=[
                pl.BlockSpec((1, 512, 512), lambda i, m: (hop, 0, 0)),
                pl.BlockSpec((1, 512, BLK), lambda i, m: (hop, 0, m[0])),
                pl.BlockSpec((512, BLK), lambda i, m: (0, 0)),
            ],
            out_specs=(whole, whole),
        ),
        compiler_params=params(60 * MB),
        name="first_slopes",
    )(member, saved, weights, cotangent)


def upstream_kernel(member, w_ref, s0, s1, s2, s3, u_ref):
    me = member[0]
    parts = []
    for d in range(NX):
        start = pl.multiple_of(lax.rem(me - d + NX, NX) * BLK, BLK)
        parts.append(w_ref[:, pl.ds(start, BLK)])
    lhs = jnp.concatenate(parts, axis=1)
    for r in range(NB):
        rhs = jnp.concatenate([s[r] for s in (s0, s1, s2, s3)], axis=0)
        u_ref[r] = jnp.dot(lhs, rhs, preferred_element_type=f32).astype(bf16)


def upstream_of(member, rows, pieces):
    whole = pl.BlockSpec((NB, BLK, BLK), lambda i, m: (0, 0, 0))
    return pl.pallas_call(
        upstream_kernel,
        out_shape=jax.ShapeDtypeStruct((NB, BLK, BLK), bf16),
        grid_spec=pltpu.PrefetchScalarGridSpec(
            num_scalar_prefetch=1,
            grid=(1,),
            in_specs=[pl.BlockSpec((BLK, 512), lambda i, m: (0, 0))] + [whole] * NX,
            out_specs=whole,
        ),
        compiler_params=params(16 * MB),
        name="upstream",
    )(member, rows, *pieces)


def weight_kernel(*refs, scale):
    *ins, out_ref = refs
    count = len(ins) // 2
    for i in range(count):
        x_ref, s_ref = ins[i], ins[count + i]
        lhs = jnp.concatenate([s_ref[r] for r in range(NB)], axis=1)
        part = jnp.dot(lhs, x_ref[0], preferred_element_type=f32)
        out_ref[i * 512 : (i + 1) * 512, :] = part.T * scale


def weight_parts(saved, slopes, scale):
    hops = sorted(slopes)
    rows = len(hops) * 512

    def at(hop):
        return pl.BlockSpec((1, 512, 512), lambda i: (hop, 0, 0))

    whole = pl.BlockSpec((NB, BLK, BLK), lambda i: (0, 0, 0))
    return pl.pallas_call(
        lambda *refs: weight_kernel(*refs, scale=scale),
        out_shape=jax.ShapeDtypeStruct((rows, BLK), f32),
        grid=(1,),
        in_specs=[at(hop) for hop in hops] + [whole] * len(hops),
        out_specs=pl.BlockSpec((rows, BLK), lambda i: (0, 0)),
        compiler_params=params(60 * MB),
        cost_estimate=cost(1),
        name="weight_parts",
    )(*[saved] * len(hops), *[slopes[hop] for hop in hops])


def total_kernel(x_ref, out_ref):
    total = x_ref[0]
    for i in range(1, x_ref.shape[0]):
        total += x_ref[i]
    out_ref[...] = total


def summed(parts):
    rows = parts.shape[0] // (NZ * NY)
    got = lax.all_to_all(parts, "dp", 0, 0, axis_index_groups=YZ_GROUPS, tiled=True)
    return pl.pallas_call(
        total_kernel,
        out_shape=jax.ShapeDtypeStruct((rows, BLK), f32),
        in_specs=[vmem()],
        out_specs=vmem(),
        compiler_params=params(8 * MB),
        cost_estimate=cost(0.5),
        name="total",
    )(got.reshape(NZ * NY, rows, BLK))


def spread_kernel(a_ref, b_ref, out_ref):
    total = (a_ref[...] + b_ref[...]).astype(bf16)
    for i in range(NZ * NY):
        out_ref[i] = total


def spread(mine):
    theirs = lax.ppermute(mine, "dp", shift(dc=1))
    shape = (NZ * NY,) + mine.shape
    return pl.pallas_call(
        spread_kernel,
        out_shape=jax.ShapeDtypeStruct(shape, bf16),
        grid=(1,),
        in_specs=[pl.BlockSpec(mine.shape, lambda i: (0, 0))] * 2,
        out_specs=pl.BlockSpec(shape, lambda i: (0, 0, 0)),
        compiler_params=params(60 * MB),
        cost_estimate=cost(0.5),
        name="spread",
    )(mine, theirs)


def collect(copies):
    whole = lax.all_to_all(copies, "dp", 0, 0, axis_index_groups=YZ_GROUPS, tiled=True)
    whole = whole.reshape(NZ * NY, -1, BLK).astype(f32)
    rows = 512 // (NZ * NY)
    first, others = whole[:, :rows], whole[:, rows:]
    return jnp.concatenate([first.reshape(1, 512, BLK), others.reshape(HOPS - 1, 512, BLK)])


def message_kernel(table, own_ref, sib_ref, a_own, a_sib, out_a, *rest):
    out_b = rest[:NZ]
    edges, acc, up, stage, stage_b, sems, out_sems, out_b_sems = rest[NZ:]
    copies = [
        pltpu.make_async_copy(a_own, edges.at[pl.ds(0, EDGES // 2)], sems.at[0]),
        pltpu.make_async_copy(a_sib, edges.at[pl.ds(EDGES // 2, EDGES // 2)], sems.at[1]),
    ]
    for copy in copies:
        copy.start()
    up[0:NB] = own_ref[...]
    up[NB : 2 * NB] = sib_ref[...]
    up[2 * NB] = jnp.zeros((BLK, BLK), bf16)

    @pl.loop(0, SLOTS // 4)
    def _(i):
        acc[pl.ds(i * 4, 4)] = jnp.zeros((4, BLK, BLK), f32)

    n_items, n_own = table[5 * ITEMS], table[5 * ITEMS + 3]

    def add_items(i):
        sums = []
        for j in range(UNROLL):
            at = i * UNROLL + j
            lhs = jnp.concatenate([up[table[3 * ITEMS + at]], up[table[4 * ITEMS + at]]], axis=1)
            rhs = jnp.concatenate([edges[table[ITEMS + at]], edges[table[2 * ITEMS + at]]], axis=0)
            sums.append(jnp.dot(lhs, rhs, preferred_element_type=f32))
        for j in range(UNROLL):
            slot = table[i * UNROLL + j]
            acc[slot] = acc[slot] + sums[j]

    early = n_own // UNROLL
    copies[0].wait()
    pl.loop(0, early)(add_items)
    copies[1].wait()
    pl.loop(early, (n_items + UNROLL - 1) // UNROLL)(add_items)

    z, y = table[5 * ITEMS + 1], table[5 * ITEMS + 2]
    sends = []
    for dz in range(NZ):
        for dy in range(NY):
            place = dz * 2 + dy // 2
            for b in range(NB):
                total = acc[(dz * NY + dy) * NB + b].astype(bf16)
                stage[dz, dy, b] = total[:HALF]
                stage_b[(place + 1) // 2 % NZ, (place + 1) % 2, dy % 2, b] = total[HALF:]
            send = pltpu.make_async_copy(
                stage.at[dz, dy],
                out_a.at[lax.rem(y + dy, NY), lax.rem(z + dz, NZ)],
                out_sems.at[dz * NY + dy],
            )
            send.start()
            sends.append(send)
        ready = [dz] if dz else []
        if dz == NZ - 1:
            ready.append(0)
        for pair in ready:
            send = pltpu.make_async_copy(stage_b.at[pair], out_b[pair], out_b_sems.at[pair])
            send.start()
            sends.append(send)
    for send in sends:
        send.wait()


def messages_of(table, own, sibling, a_own, a_sib):
    hbm = pl.BlockSpec(memory_space=pltpu.HBM)
    return pl.pallas_call(
        message_kernel,
        out_shape=(jax.ShapeDtypeStruct((NY, NZ, NB, HALF, BLK), bf16),)
        + (jax.ShapeDtypeStruct(PAIR, bf16),) * NZ,
        in_specs=[pl.BlockSpec(memory_space=pltpu.SMEM), vmem(), vmem(), hbm, hbm],
        out_specs=(hbm,) * (NZ + 1),
        scratch_shapes=[
            pltpu.VMEM((EDGES, BLK, BLK), bf16),
            pltpu.VMEM((SLOTS + 1, BLK, BLK), f32),
            pltpu.VMEM((2 * NB + 1, BLK, BLK), bf16),
            pltpu.VMEM((NZ, NY, NB, HALF, BLK), bf16),
            pltpu.VMEM((NZ,) + PAIR, bf16),
            pltpu.SemaphoreType.DMA((2,)),
            pltpu.SemaphoreType.DMA((NZ * NY,)),
            pltpu.SemaphoreType.DMA((NZ,)),
        ],
        compiler_params=params(60 * MB),
        cost_estimate=cost(6),
        name="messages",
    )(table, own, sibling, a_own, a_sib)


def arrivals(from_z, from_y, r):
    first = from_z[0, r].astype(f32)
    for i in range(1, NZ):
        first += from_z[i, r].astype(f32)
    second = from_y[0][r].astype(f32)
    for part in from_y[1:]:
        second += part[r].astype(f32)
    return jnp.concatenate([first, second], axis=0)


def update_kernel(from_z, *refs):
    from_y, (grad_ref, d_ref, new_ref, slope_ref) = refs[:NY], refs[NY:]
    for r in range(NB):
        grad = grad_ref[r] + arrivals(from_z, from_y, r)
        new_ref[r] = grad
        slope_ref[r] = (grad * d_ref[r]).astype(bf16)


def update(from_z, from_y, grad, factor):
    return pl.pallas_call(
        update_kernel,
        out_shape=(
            jax.ShapeDtypeStruct((NB, BLK, BLK), f32),
            jax.ShapeDtypeStruct((NB, BLK, BLK), bf16),
        ),
        in_specs=[vmem()] * (NY + 3),
        out_specs=(vmem(), vmem()),
        compiler_params=params(16 * MB),
        cost_estimate=cost(1),
        name="update",
    )(from_z, *from_y, grad, factor)


def last_kernel(from_z, *refs):
    from_y, (grad_ref, out_ref) = refs[:NY], refs[NY:]
    for r in range(NB):
        grad = grad_ref[r] + arrivals(from_z, from_y, r)
        out_ref[r * BLK : (r + 1) * BLK, :] = grad.T.astype(bf16)


def last_update(from_z, from_y, grad):
    return pl.pallas_call(
        last_kernel,
        out_shape=jax.ShapeDtypeStruct((NB * BLK, BLK), bf16),
        in_specs=[vmem()] * (NY + 2),
        out_specs=vmem(),
        compiler_params=params(16 * MB),
        cost_estimate=cost(1),
        name="last_update",
    )(from_z, *from_y, grad)


def plus(a, b):
    return (a.astype(f32) + b.astype(f32)).astype(bf16)


def fetch(held, sems, *sources):
    copies = [
        pltpu.make_async_copy(q, held.at[i], sems.at[i]) for i, q in enumerate(sources)
    ]
    for copy in copies:
        copy.start()
    for copy in copies:
        copy.wait()


def step_kernel(q_up, q_down, got_up, got_down, up, down, held, sems):
    fetch(held, sems, q_up, q_down)
    up[...] = plus(held[0], got_up[...])
    down[...] = plus(held[1], got_down[...])


def final_kernel(q_up, q_down, got_up, got_down, up, down, keep, held, sems):
    fetch(held, sems, q_up, q_down)
    up[...] = plus(held[0, 1], got_up[1])
    down[...] = plus(held[1, 0], got_down[0])
    keep[0] = held[1, 1].astype(f32) + got_down[1].astype(f32)
    keep[1] = held[0, 0].astype(f32) + got_up[0].astype(f32)


def step(q_up, q_down, got_up, got_down, final):
    hbm = pl.BlockSpec(memory_space=pltpu.HBM)
    sent = jax.ShapeDtypeStruct(PAIR[1:] if final else PAIR, bf16)
    kept = (jax.ShapeDtypeStruct(PAIR, f32),) if final else ()
    return pl.pallas_call(
        final_kernel if final else step_kernel,
        out_shape=(sent, sent) + kept,
        in_specs=[hbm, hbm, vmem(), vmem()],
        out_specs=(vmem(),) * (3 if final else 2),
        scratch_shapes=[pltpu.VMEM((2,) + PAIR, bf16), pltpu.SemaphoreType.DMA((2,))],
        compiler_params=params(4 * MB),
        cost_estimate=cost(0.5),
        name="final_step" if final else "step",
    )(q_up, q_down, got_up, got_down)


def ring_end_kernel(keep, last_up, last_down, *out):
    for i, last in enumerate((last_up, last_down)):
        total = keep[i] + last[...].astype(f32)
        for j in range(NY // 2):
            at = out[i * (NY // 2) + j]
            at[...] = total[j].astype(at.dtype)


def ring_end(keep, last_up, last_down):
    shape = (NB, HALF, BLK)
    return pl.pallas_call(
        ring_end_kernel,
        out_shape=(jax.ShapeDtypeStruct(shape, f32),)
        + (jax.ShapeDtypeStruct(shape, bf16),) * (NY - 1),
        in_specs=[vmem()] * 3,
        out_specs=(vmem(),) * NY,
        compiler_params=params(4 * MB),
        cost_estimate=cost(0.5),
        name="ring_end",
    )(keep, last_up, last_down)


def ring(q, tie):
    ahead, back = shift(dz=1), shift(dz=-1)
    up, down = q[NZ // 2], q[NZ // 2 + 1]
    keep = None
    for k in range(1, NZ // 2):
        got_up = lax.ppermute(up, "dp", ahead)
        got_down = lax.ppermute(down, "dp", back)
        got_up, got_down = tie(k, got_up, got_down)
        args = (q[NZ // 2 - k], q[(NZ // 2 + 1 + k) % NZ], got_up, got_down)
        up, down, *keep = step(*args, k == NZ // 2 - 1)
    last_up = lax.ppermute(up, "dp", ahead)
    last_down = lax.ppermute(down, "dp", back)
    last_up, last_down = tie(NZ // 2, last_up, last_down)
    return ring_end(*keep, last_up, last_down)


def sum_y_kernel(x_ref, out_ref, held, made, sems, out_sems):
    copies, sends = [], []
    for i in range(NZ // 2):
        two = pl.ds(2 * i, 2)
        copies.append(pltpu.make_async_copy(x_ref.at[:, two], held.at[:, two], sems.at[i]))
        sends.append(pltpu.make_async_copy(made.at[two], out_ref.at[two], out_sems.at[i]))
    for copy in copies:
        copy.start()
    for i in range(NZ // 2):
        two = slice(2 * i, 2 * i + 2)
        copies[i].wait()
        total = held[0, two].astype(f32)
        for j in range(1, NY):
            total += held[j, two].astype(f32)
        made[two] = total.astype(bf16)
        sends[i].start()
    for send in sends:
        send.wait()


def sum_y(x):
    hbm = pl.BlockSpec(memory_space=pltpu.HBM)
    return pl.pallas_call(
        sum_y_kernel,
        out_shape=jax.ShapeDtypeStruct(x.shape[1:], bf16),
        in_specs=[hbm],
        out_specs=hbm,
        scratch_shapes=[
            pltpu.VMEM(x.shape, bf16),
            pltpu.VMEM(x.shape[1:], bf16),
            pltpu.SemaphoreType.DMA((NZ // 2,)),
            pltpu.SemaphoreType.DMA((NZ // 2,)),
        ],
        compiler_params=params(60 * MB),
        cost_estimate=cost(SUM_Y_COST),
        name="sum_y",
    )(x)


def exchange(out_a, out_b, beside=None):
    by_y = lax.all_to_all(out_a, "dp", 0, 0, axis_index_groups=Y_GROUPS, tiled=True)
    made = {"sums": sum_y(by_y), "beside": beside}

    def tie(k, up, down):
        if k == STIE:
            up, down, made["sums"] = lax.optimization_barrier((up, down, made["sums"]))
        if k == 1 and beside is not None:
            up, down, made["beside"] = lax.optimization_barrier((up, down, beside))
        return up, down

    own, *others = ring(out_b, tie)
    from_z = lax.all_to_all(made["sums"], "dp", 0, 0, axis_index_groups=Z_GROUPS, tiled=True)
    from_y = [own] + [lax.ppermute(x, "dp", shift(dy=d + 1)) for d, x in enumerate(others)]
    return from_z, from_y, made["beside"]


def routing(edge_rows, edge_cols, edge_counts, block_owner, z, y, c):
    live = jnp.arange(EDGES // 2, dtype=jnp.int32) < edge_counts[0]
    code = jnp.where(live, block_owner[edge_cols], -1)
    mine = jnp.stack([code, edge_rows])
    theirs = lax.ppermute(mine, "dp", shift(dc=1))
    code = jnp.concatenate([mine[0], theirs[0]])
    rows = jnp.concatenate([mine[1], theirs[1] + NB])
    dev = code // NB
    used = (code >= 0) & (dev % NC == c)
    y_to, z_to = (dev // NC) % NY, dev // (NC * NY)
    slot = jnp.where(used, ((z_to - z + NZ) % NZ * NY + (y_to - y + NY) % NY) * NB + code % NB, SLOTS)
    ids = jnp.arange(EDGES, dtype=jnp.int32)
    key = jnp.where(used, slot + SLOTS * (ids // (EDGES // 2)), 2 * SLOTS)
    keys = jnp.arange(2 * SLOTS, dtype=jnp.int32)
    same = (key[:, None] == key[None, :]) & (ids[None, :] < ids[:, None])
    rank = jnp.sum(same.astype(jnp.int32), axis=1)
    hit = (key[:, None] == keys[None, :]).astype(jnp.int32)
    pairs = (jnp.sum(hit, axis=0) + 1) // 2
    base = jnp.sum(jnp.where(keys[None, :] < keys[:, None], pairs[None, :], 0), axis=1)
    item = jnp.where(used, jnp.sum(hit * base[None, :], axis=1) + rank // 2, -1)
    side = rank % 2
    place = jnp.arange(ITEMS, dtype=jnp.int32)
    at = [
        (place[:, None] == item[None, :]) & (side[None, :] == s) for s in range(2)
    ]

    def pick(mask, values, default):
        return jnp.sum(jnp.where(mask, values[None, :] - default, 0), axis=1) + default

    return jnp.concatenate(
        [
            pick(at[0], slot, SLOTS),
            pick(at[0], ids, 0),
            pick(at[1], ids, 0),
            pick(at[0], rows, 2 * NB),
            pick(at[1], rows, 2 * NB),
            jnp.stack([jnp.sum(pairs), z, y, jnp.sum(pairs[:SLOTS])]),
        ]
    ).astype(jnp.int32)


def on_device(
    cotangent, saved_inputs, weights, edge_values, edge_rows, edge_cols, edge_counts, block_owner
):
    scale = 1.0 / math.sqrt(saved_inputs.shape[1] * lax.axis_size("dp"))
    dp = lax.axis_index("dp")
    z, y, c = dp // (NY * NC), dp // NC % NY, dp % NC
    group = lax.axis_index("group")
    member = jnp.full((1,), group, jnp.int32)

    edges_sib = lax.ppermute(edge_values, "dp", shift(dc=1))
    table = routing(edge_rows, edge_cols, edge_counts, block_owner, z, y, c)
    grad, slopes = first_slopes(member, saved_inputs, weights, cotangent)
    factor = [factors(member, saved_inputs, weights, h) for h in range(HOPS - 1)]

    my_rows = [
        lax.dynamic_slice(weights, (h, group * BLK, 0), (1, BLK, 512))[0] for h in range(HOPS)
    ]
    kept = {}
    for hop in reversed(range(HOPS)):
        pieces = [slopes] + [
            lax.ppermute(slopes, "group", [(i, (i + d) % NX) for i in range(NX)])
            for d in range(1, NX)
        ]
        kept[hop] = slopes
        own = upstream_of(member, my_rows[hop], pieces)
        sibling = lax.ppermute(own, "dp", shift(dc=1))
        beside = None
        if hop == 1:
            sibling, kept[hop] = lax.optimization_barrier((sibling, kept[hop]))
            beside = summed(weight_parts(saved_inputs, kept, scale))
        if hop == 0:
            last = summed(weight_parts(saved_inputs, {0: slopes}, scale))
            copies = spread(jnp.concatenate([last, beside_sums], axis=0))
            sibling, copies = lax.optimization_barrier((sibling, copies))
            beside = collect(copies)
        out_a, *out_b = messages_of(table, own, sibling, edge_values, edges_sib)
        from_z, from_y, beside = exchange(out_a, out_b, beside)
        if hop:
            beside_sums = beside
            grad, slopes = update(from_z, from_y, grad, factor[hop - 1])
        else:
            result = last_update(from_z, from_y, grad)
    return result, beside


def solution(mesh):
    in_specs = (
        P("dp", "group"),
        P(None, "dp", None),
        P(),
        P("dp", None, None),
        P("dp"),
        P("dp"),
        P("dp"),
        P(),
    )
    out_specs = (P("dp", "group"), P(None, None, "group"))
    return jax.shard_map(
        on_device, mesh=mesh, in_specs=in_specs, out_specs=out_specs, check_vma=False
    )
```

```python
import math

import jax
import jax.numpy as jnp
from jax import lax
from jax.experimental import pallas as pl
from jax.experimental.pallas import tpu as pltpu
from jax.sharding import PartitionSpec as P

BLK = 128
HOPS = 3
NZ, NY, NC = 8, 4, 2
NX = 4
NB = 4
SLOTS = NZ * NY * NB
EDGES = 256
UNROLL = 8
ITEMS = 264
HALF = 64

bf16 = jnp.bfloat16
f32 = jnp.float32
MB = 1 << 20


def index_of(z, y, c):
    return ((z % NZ) * NY + (y % NY)) * NC + c


def shift(dz=0, dy=0, dc=0):
    return [
        (index_of(z, y, c), index_of(z + dz, y + dy, c ^ dc))
        for z in range(NZ)
        for y in range(NY)
        for c in range(NC)
    ]


Y_GROUPS = [[index_of(z, y, c) for y in range(NY)] for z in range(NZ) for c in range(NC)]
Z_GROUPS = [[index_of(z, y, c) for z in range(NZ)] for y in range(NY) for c in range(NC)]


YZ_GROUPS = [[index_of(z, y, c) for z in range(NZ) for y in range(NY)] for c in range(NC)]
PAIR = (2, NY // 2, NB, HALF, BLK)
SUM_Y_COST = 1
SUMS = 512 // (NZ * NY)
ROWS = NB * HALF + 2 * SUMS
STIE = 4


def cost(us):
    return pl.CostEstimate(flops=0, bytes_accessed=int(us * 3_300_000), transcendentals=0)


def silu_slope(value):
    sigma = jax.nn.sigmoid(value)
    return sigma * (1.0 + value * (1.0 - sigma))


def vmem():
    return pl.BlockSpec(memory_space=pltpu.VMEM)


def params(limit):
    return pltpu.CompilerParams(vmem_limit_bytes=limit)


def factor_kernel(member, x_ref, w_ref, d_ref):
    for r in range(NB):
        z = jnp.dot(x_ref[0, r * BLK : (r + 1) * BLK, :], w_ref[0], preferred_element_type=f32)
        d_ref[r] = silu_slope(z.T)


def factors(member, saved, weights, hop):
    return pl.pallas_call(
        factor_kernel,
        out_shape=jax.ShapeDtypeStruct((NB, BLK, BLK), f32),
        grid_spec=pltpu.PrefetchScalarGridSpec(
            num_scalar_prefetch=1,
            grid=(1,),
            in_specs=[
                pl.BlockSpec((1, 512, 512), lambda i, m: (hop, 0, 0)),
                pl.BlockSpec((1, 512, BLK), lambda i, m: (hop, 0, m[0])),
            ],
            out_specs=pl.BlockSpec((NB, BLK, BLK), lambda i, m: (0, 0, 0)),
        ),
        compiler_params=params(60 * MB),
        name="factors",
    )(member, saved, weights)


def first_kernel(member, x_ref, w_ref, cot_ref, grad_ref, slope_ref):
    for r in range(NB):
        rows = slice(r * BLK, (r + 1) * BLK)
        z = jnp.dot(x_ref[0, rows, :], w_ref[0], preferred_element_type=f32)
        grad = cot_ref[rows, :].astype(f32).T
        grad_ref[r] = grad
        slope_ref[r] = (grad * silu_slope(z.T)).astype(bf16)


def first_slopes(member, saved, weights, cotangent):
    hop = HOPS - 1
    whole = pl.BlockSpec((NB, BLK, BLK), lambda i, m: (0, 0, 0))
    return pl.pallas_call(
        first_kernel,
        out_shape=(
            jax.ShapeDtypeStruct((NB, BLK, BLK), f32),
            jax.ShapeDtypeStruct((NB, BLK, BLK), bf16),
        ),
        grid_spec=pltpu.PrefetchScalarGridSpec(
            num_scalar_prefetch=1,
            grid=(1,),
            in_specs=[
                pl.BlockSpec((1, 512, 512), lambda i, m: (hop, 0, 0)),
                pl.BlockSpec((1, 512, BLK), lambda i, m: (hop, 0, m[0])),
                pl.BlockSpec((512, BLK), lambda i, m: (0, 0)),
            ],
            out_specs=(whole, whole),
        ),
        compiler_params=params(60 * MB),
        name="first_slopes",
    )(member, saved, weights, cotangent)


def upstream_kernel(member, w_ref, s0, s1, s2, s3, u_ref):
    me = member[0]
    parts = []
    for d in range(NX):
        start = pl.multiple_of(lax.rem(me - d + NX, NX) * BLK, BLK)
        parts.append(w_ref[:, pl.ds(start, BLK)])
    lhs = jnp.concatenate(parts, axis=1)
    for r in range(NB):
        rhs = jnp.concatenate([s[r] for s in (s0, s1, s2, s3)], axis=0)
        u_ref[r] = jnp.dot(lhs, rhs, preferred_element_type=f32).astype(bf16)


def upstream_of(member, rows, pieces):
    whole = pl.BlockSpec((NB, BLK, BLK), lambda i, m: (0, 0, 0))
    return pl.pallas_call(
        upstream_kernel,
        out_shape=jax.ShapeDtypeStruct((NB, BLK, BLK), bf16),
        grid_spec=pltpu.PrefetchScalarGridSpec(
            num_scalar_prefetch=1,
            grid=(1,),
            in_specs=[pl.BlockSpec((BLK, 512), lambda i, m: (0, 0))] + [whole] * NX,
            out_specs=whole,
        ),
        compiler_params=params(16 * MB),
        name="upstream",
    )(member, rows, *pieces)


def split(x):
    high = x.astype(bf16)
    return high, (x - high.astype(f32)).astype(bf16)


def joined(x):
    return x[:SUMS].astype(f32) + x[SUMS:].astype(f32)


def weight_kernel(x_ref, s_ref, out_ref, *, scale):
    lhs = jnp.concatenate([s_ref[r] for r in range(NB)], axis=1)
    part = jnp.dot(lhs, x_ref[0], preferred_element_type=f32).T * scale
    high, low = split(part)
    for z in range(NZ):
        for y in range(NY):
            start = (z * NY + y) * SUMS
            out_ref[y, z, :SUMS] = high[start : start + SUMS]
            out_ref[y, z, SUMS:] = low[start : start + SUMS]


def weight_part(saved, slopes, hop, scale):
    shape = (NY, NZ, 2 * SUMS, BLK)
    return pl.pallas_call(
        lambda *refs: weight_kernel(*refs, scale=scale),
        out_shape=jax.ShapeDtypeStruct(shape, bf16),
        grid=(1,),
        in_specs=[
            pl.BlockSpec((1, 512, 512), lambda i: (hop, 0, 0)),
            pl.BlockSpec((NB, BLK, BLK), lambda i: (0, 0, 0)),
        ],
        out_specs=pl.BlockSpec(shape, lambda i: (0, 0, 0, 0)),
        compiler_params=params(60 * MB),
        cost_estimate=cost(1),
        name="weight_part",
    )(saved, slopes)


def spread_kernel(a_ref, b_ref, out_ref):
    total = (a_ref[...] + b_ref[...]).astype(bf16)
    for i in range(NZ * NY):
        out_ref[i] = total


def spread(mine):
    theirs = lax.ppermute(mine, "dp", shift(dc=1))
    shape = (NZ * NY,) + mine.shape
    return pl.pallas_call(
        spread_kernel,
        out_shape=jax.ShapeDtypeStruct(shape, bf16),
        grid=(1,),
        in_specs=[pl.BlockSpec(mine.shape, lambda i: (0, 0))] * 2,
        out_specs=pl.BlockSpec(shape, lambda i: (0, 0, 0)),
        compiler_params=params(60 * MB),
        cost_estimate=cost(0.5),
        name="spread",
    )(mine, theirs)


def collect(copies):
    whole = lax.all_to_all(copies, "dp", 0, 0, axis_index_groups=YZ_GROUPS, tiled=True)
    whole = whole.reshape(NZ * NY, HOPS, SUMS, BLK).transpose(1, 0, 2, 3)
    return whole.reshape(HOPS, 512, BLK).astype(f32)


def message_kernel(table, own_ref, sib_ref, a_own, a_sib, weight_ref, out_a, *rest):
    out_b = rest[:NZ]
    edges, acc, up, stage, stage_b, sems, out_sems, out_b_sems = rest[NZ:]
    copies = [
        pltpu.make_async_copy(a_own, edges.at[pl.ds(0, EDGES // 2)], sems.at[0]),
        pltpu.make_async_copy(a_sib, edges.at[pl.ds(EDGES // 2, EDGES // 2)], sems.at[1]),
    ]
    copies[0].start()
    up[0:NB] = own_ref[...]
    up[NB : 2 * NB] = sib_ref[...]
    up[2 * NB] = jnp.zeros((BLK, BLK), bf16)

    @pl.loop(0, SLOTS // 4)
    def _(i):
        acc[pl.ds(i * 4, 4)] = jnp.zeros((4, BLK, BLK), f32)

    n_items, n_own = table[5 * ITEMS], table[5 * ITEMS + 3]

    def add_items(i):
        sums = []
        for j in range(UNROLL):
            at = i * UNROLL + j
            lhs = jnp.concatenate([up[table[3 * ITEMS + at]], up[table[4 * ITEMS + at]]], axis=1)
            rhs = jnp.concatenate([edges[table[ITEMS + at]], edges[table[2 * ITEMS + at]]], axis=0)
            sums.append(jnp.dot(lhs, rhs, preferred_element_type=f32))
        for j in range(UNROLL):
            slot = table[i * UNROLL + j]
            acc[slot] = acc[slot] + sums[j]

    early = n_own // UNROLL
    copies[0].wait()
    copies[1].start()
    weight_copy = pltpu.make_async_copy(
        weight_ref, out_a.at[:, :, pl.ds(NB * HALF, 2 * SUMS)], sems.at[2]
    )
    weight_copy.start()
    pl.loop(0, early)(add_items)
    copies[1].wait()
    pl.loop(early, (n_items + UNROLL - 1) // UNROLL)(add_items)

    z, y = table[5 * ITEMS + 1], table[5 * ITEMS + 2]
    sends = []
    for dz in range(NZ):
        for dy in range(NY):
            place = dz * 2 + dy // 2
            for b in range(NB):
                total = acc[(dz * NY + dy) * NB + b].astype(bf16)
                stage[dz, dy, b * HALF : (b + 1) * HALF] = total[:HALF]
                stage_b[(place + 1) // 2 % NZ, (place + 1) % 2, dy % 2, b] = total[HALF:]
            send = pltpu.make_async_copy(
                stage.at[dz, dy],
                out_a.at[lax.rem(y + dy, NY), lax.rem(z + dz, NZ), pl.ds(0, NB * HALF)],
                out_sems.at[dz * NY + dy],
            )
            send.start()
            sends.append(send)
        ready = [dz] if dz else []
        if dz == NZ - 1:
            ready.append(0)
        for pair in ready:
            send = pltpu.make_async_copy(stage_b.at[pair], out_b[pair], out_b_sems.at[pair])
            send.start()
            sends.append(send)
    for send in sends:
        send.wait()
    weight_copy.wait()


def messages_of(table, own, sibling, a_own, a_sib, weight):
    hbm = pl.BlockSpec(memory_space=pltpu.HBM)
    return pl.pallas_call(
        message_kernel,
        out_shape=(jax.ShapeDtypeStruct((NY, NZ, ROWS, BLK), bf16),)
        + (jax.ShapeDtypeStruct(PAIR, bf16),) * NZ,
        in_specs=[pl.BlockSpec(memory_space=pltpu.SMEM), vmem(), vmem(), hbm, hbm, hbm],
        out_specs=(hbm,) * (NZ + 1),
        scratch_shapes=[
            pltpu.VMEM((EDGES, BLK, BLK), bf16),
            pltpu.VMEM((SLOTS + 1, BLK, BLK), f32),
            pltpu.VMEM((2 * NB + 1, BLK, BLK), bf16),
            pltpu.VMEM((NZ, NY, NB * HALF, BLK), bf16),
            pltpu.VMEM((NZ,) + PAIR, bf16),
            pltpu.SemaphoreType.DMA((3,)),
            pltpu.SemaphoreType.DMA((NZ * NY,)),
            pltpu.SemaphoreType.DMA((NZ,)),
        ],
        compiler_params=params(60 * MB),
        cost_estimate=cost(6),
        name="messages",
    )(table, own, sibling, a_own, a_sib, weight)


def arrivals(from_z, from_y, r):
    rows = slice(r * HALF, (r + 1) * HALF)
    first = from_z[0, rows].astype(f32)
    for i in range(1, NZ):
        first += from_z[i, rows].astype(f32)
    second = from_y[0][r].astype(f32)
    for part in from_y[1:]:
        second += part[r].astype(f32)
    return jnp.concatenate([first, second], axis=0)


def weight_sums(from_z):
    total = joined(from_z[0, NB * HALF :])
    for i in range(1, NZ):
        total += joined(from_z[i, NB * HALF :])
    return total


def update_kernel(from_z, *refs):
    from_y, (grad_ref, d_ref, new_ref, slope_ref, sums_ref) = refs[:NY], refs[NY:]
    for r in range(NB):
        grad = grad_ref[r] + arrivals(from_z, from_y, r)
        new_ref[r] = grad
        slope_ref[r] = (grad * d_ref[r]).astype(bf16)
    sums_ref[...] = weight_sums(from_z)


def update(from_z, from_y, grad, factor):
    return pl.pallas_call(
        update_kernel,
        out_shape=(
            jax.ShapeDtypeStruct((NB, BLK, BLK), f32),
            jax.ShapeDtypeStruct((NB, BLK, BLK), bf16),
            jax.ShapeDtypeStruct((SUMS, BLK), f32),
        ),
        in_specs=[vmem()] * (NY + 3),
        out_specs=(vmem(),) * 3,
        compiler_params=params(16 * MB),
        cost_estimate=cost(1),
        name="update",
    )(from_z, *from_y, grad, factor)


def last_kernel(from_z, *refs):
    from_y, (grad_ref, out_ref) = refs[:NY], refs[NY:]
    for r in range(NB):
        grad = grad_ref[r] + arrivals(from_z, from_y, r)
        out_ref[r * BLK : (r + 1) * BLK, :] = grad.T.astype(bf16)


def last_update(from_z, from_y, grad):
    return pl.pallas_call(
        last_kernel,
        out_shape=jax.ShapeDtypeStruct((NB * BLK, BLK), bf16),
        in_specs=[vmem()] * (NY + 2),
        out_specs=vmem(),
        compiler_params=params(16 * MB),
        cost_estimate=cost(1),
        name="last_update",
    )(from_z, *from_y, grad)


def last_sums_kernel(from_z, out_ref):
    out_ref[...] = weight_sums(from_z)


def last_sums(from_z):
    return pl.pallas_call(
        last_sums_kernel,
        out_shape=jax.ShapeDtypeStruct((SUMS, BLK), f32),
        grid=(1,),
        in_specs=[pl.BlockSpec((NZ, ROWS, BLK), lambda i: (0, 0, 0))],
        out_specs=pl.BlockSpec((SUMS, BLK), lambda i: (0, 0)),
        compiler_params=params(16 * MB),
        cost_estimate=cost(0.5),
        name="last_sums",
    )(from_z)


def plus(a, b):
    return (a.astype(f32) + b.astype(f32)).astype(bf16)


def fetch(held, sems, *sources):
    copies = [
        pltpu.make_async_copy(q, held.at[i], sems.at[i]) for i, q in enumerate(sources)
    ]
    for copy in copies:
        copy.start()
    for copy in copies:
        copy.wait()


def step_kernel(q_up, q_down, got_up, got_down, up, down, held, sems):
    fetch(held, sems, q_up, q_down)
    up[...] = plus(held[0], got_up[...])
    down[...] = plus(held[1], got_down[...])


def final_kernel(q_up, q_down, got_up, got_down, up, down, keep, held, sems):
    fetch(held, sems, q_up, q_down)
    up[...] = plus(held[0, 1], got_up[1])
    down[...] = plus(held[1, 0], got_down[0])
    keep[0] = held[1, 1].astype(f32) + got_down[1].astype(f32)
    keep[1] = held[0, 0].astype(f32) + got_up[0].astype(f32)


def step(q_up, q_down, got_up, got_down, final):
    hbm = pl.BlockSpec(memory_space=pltpu.HBM)
    sent = jax.ShapeDtypeStruct(PAIR[1:] if final else PAIR, bf16)
    kept = (jax.ShapeDtypeStruct(PAIR, f32),) if final else ()
    return pl.pallas_call(
        final_kernel if final else step_kernel,
        out_shape=(sent, sent) + kept,
        in_specs=[hbm, hbm, vmem(), vmem()],
        out_specs=(vmem(),) * (3 if final else 2),
        scratch_shapes=[pltpu.VMEM((2,) + PAIR, bf16), pltpu.SemaphoreType.DMA((2,))],
        compiler_params=params(4 * MB),
        cost_estimate=cost(0.5),
        name="final_step" if final else "step",
    )(q_up, q_down, got_up, got_down)


def ring_end_kernel(keep, last_up, last_down, *out):
    for i, last in enumerate((last_up, last_down)):
        total = keep[i] + last[...].astype(f32)
        for j in range(NY // 2):
            at = out[i * (NY // 2) + j]
            at[...] = total[j].astype(at.dtype)


def ring_end(keep, last_up, last_down):
    shape = (NB, HALF, BLK)
    return pl.pallas_call(
        ring_end_kernel,
        out_shape=(jax.ShapeDtypeStruct(shape, f32),)
        + (jax.ShapeDtypeStruct(shape, bf16),) * (NY - 1),
        in_specs=[vmem()] * 3,
        out_specs=(vmem(),) * NY,
        compiler_params=params(4 * MB),
        cost_estimate=cost(0.5),
        name="ring_end",
    )(keep, last_up, last_down)


def ring(q, tie):
    ahead, back = shift(dz=1), shift(dz=-1)
    up, down = q[NZ // 2], q[NZ // 2 + 1]
    keep = None
    for k in range(1, NZ // 2):
        got_up = lax.ppermute(up, "dp", ahead)
        got_down = lax.ppermute(down, "dp", back)
        got_up, got_down = tie(k, got_up, got_down)
        args = (q[NZ // 2 - k], q[(NZ // 2 + 1 + k) % NZ], got_up, got_down)
        up, down, *keep = step(*args, k == NZ // 2 - 1)
    last_up = lax.ppermute(up, "dp", ahead)
    last_down = lax.ppermute(down, "dp", back)
    last_up, last_down = tie(NZ // 2, last_up, last_down)
    return ring_end(*keep, last_up, last_down)


def sum_y_kernel(x_ref, out_ref, held, made, sems, out_sems):
    copies, sends = [], []
    for i in range(NZ // 2):
        two = pl.ds(2 * i, 2)
        copies.append(pltpu.make_async_copy(x_ref.at[:, two], held.at[:, two], sems.at[i]))
        sends.append(pltpu.make_async_copy(made.at[two], out_ref.at[two], out_sems.at[i]))
    for copy in copies:
        copy.start()
    for i in range(NZ // 2):
        two = slice(2 * i, 2 * i + 2)
        copies[i].wait()
        total = held[0, two].astype(f32)
        for j in range(1, NY):
            total += held[j, two].astype(f32)
        made[two] = total.astype(bf16)
        for j in (2 * i, 2 * i + 1):
            part = joined(held[0, j, NB * HALF :])
            for k in range(1, NY):
                part += joined(held[k, j, NB * HALF :])
            high, low = split(part)
            made[j, NB * HALF : NB * HALF + SUMS] = high
            made[j, NB * HALF + SUMS :] = low
        sends[i].start()
    for send in sends:
        send.wait()


def sum_y(x):
    hbm = pl.BlockSpec(memory_space=pltpu.HBM)
    return pl.pallas_call(
        sum_y_kernel,
        out_shape=jax.ShapeDtypeStruct(x.shape[1:], bf16),
        in_specs=[hbm],
        out_specs=hbm,
        scratch_shapes=[
            pltpu.VMEM(x.shape, bf16),
            pltpu.VMEM(x.shape[1:], bf16),
            pltpu.SemaphoreType.DMA((NZ // 2,)),
            pltpu.SemaphoreType.DMA((NZ // 2,)),
        ],
        compiler_params=params(60 * MB),
        cost_estimate=cost(SUM_Y_COST),
        name="sum_y",
    )(x)


def exchange(out_a, out_b):
    by_y = lax.all_to_all(out_a, "dp", 0, 0, axis_index_groups=Y_GROUPS, tiled=True)
    made = {"sums": sum_y(by_y)}

    def tie(k, up, down):
        if k == STIE:
            up, down, made["sums"] = lax.optimization_barrier((up, down, made["sums"]))
        return up, down

    own, *others = ring(out_b, tie)
    from_z = lax.all_to_all(made["sums"], "dp", 0, 0, axis_index_groups=Z_GROUPS, tiled=True)
    from_y = [own] + [lax.ppermute(x, "dp", shift(dy=d + 1)) for d, x in enumerate(others)]
    return from_z, from_y


def routing(edge_rows, edge_cols, edge_counts, block_owner, z, y, c):
    live = jnp.arange(EDGES // 2, dtype=jnp.int32) < edge_counts[0]
    code = jnp.where(live, block_owner[edge_cols], -1)
    mine = jnp.stack([code, edge_rows])
    theirs = lax.ppermute(mine, "dp", shift(dc=1))
    code = jnp.concatenate([mine[0], theirs[0]])
    rows = jnp.concatenate([mine[1], theirs[1] + NB])
    dev = code // NB
    used = (code >= 0) & (dev % NC == c)
    y_to, z_to = (dev // NC) % NY, dev // (NC * NY)
    slot = jnp.where(used, ((z_to - z + NZ) % NZ * NY + (y_to - y + NY) % NY) * NB + code % NB, SLOTS)
    ids = jnp.arange(EDGES, dtype=jnp.int32)
    key = jnp.where(used, slot + SLOTS * (ids // (EDGES // 2)), 2 * SLOTS)
    keys = jnp.arange(2 * SLOTS, dtype=jnp.int32)
    same = (key[:, None] == key[None, :]) & (ids[None, :] < ids[:, None])
    rank = jnp.sum(same.astype(jnp.int32), axis=1)
    hit = (key[:, None] == keys[None, :]).astype(jnp.int32)
    pairs = (jnp.sum(hit, axis=0) + 1) // 2
    base = jnp.sum(jnp.where(keys[None, :] < keys[:, None], pairs[None, :], 0), axis=1)
    item = jnp.where(used, jnp.sum(hit * base[None, :], axis=1) + rank // 2, -1)
    side = rank % 2
    place = jnp.arange(ITEMS, dtype=jnp.int32)
    at = [
        (place[:, None] == item[None, :]) & (side[None, :] == s) for s in range(2)
    ]

    def pick(mask, values, default):
        return jnp.sum(jnp.where(mask, values[None, :] - default, 0), axis=1) + default

    return jnp.concatenate(
        [
            pick(at[0], slot, SLOTS),
            pick(at[0], ids, 0),
            pick(at[1], ids, 0),
            pick(at[0], rows, 2 * NB),
            pick(at[1], rows, 2 * NB),
            jnp.stack([jnp.sum(pairs), z, y, jnp.sum(pairs[:SLOTS])]),
        ]
    ).astype(jnp.int32)


def on_device(
    cotangent, saved_inputs, weights, edge_values, edge_rows, edge_cols, edge_counts, block_owner
):
    scale = 1.0 / math.sqrt(saved_inputs.shape[1] * lax.axis_size("dp"))
    dp = lax.axis_index("dp")
    z, y, c = dp // (NY * NC), dp // NC % NY, dp % NC
    group = lax.axis_index("group")
    member = jnp.full((1,), group, jnp.int32)

    edges_sib = lax.ppermute(edge_values, "dp", shift(dc=1))
    table = routing(edge_rows, edge_cols, edge_counts, block_owner, z, y, c)
    grad, slopes = first_slopes(member, saved_inputs, weights, cotangent)
    factor = [factors(member, saved_inputs, weights, h) for h in range(HOPS - 1)]

    my_rows = [
        lax.dynamic_slice(weights, (h, group * BLK, 0), (1, BLK, 512))[0] for h in range(HOPS)
    ]
    sums = [None] * HOPS
    for hop in reversed(range(HOPS)):
        pieces = [slopes] + [
            lax.ppermute(slopes, "group", [(i, (i + d) % NX) for i in range(NX)])
            for d in range(1, NX)
        ]
        weight = weight_part(saved_inputs, slopes, hop, scale)
        own = upstream_of(member, my_rows[hop], pieces)
        sibling = lax.ppermute(own, "dp", shift(dc=1))
        out_a, *out_b = messages_of(table, own, sibling, edge_values, edges_sib, weight)
        from_z, from_y = exchange(out_a, out_b)
        if hop:
            grad, slopes, sums[hop] = update(from_z, from_y, grad, factor[hop - 1])
    result = last_update(from_z, from_y, grad)
    sums[0] = last_sums(from_z)
    return result, collect(spread(jnp.concatenate(sums, axis=0)))


def solution(mesh):
    in_specs = (
        P("dp", "group"),
        P(None, "dp", None),
        P(),
        P("dp", None, None),
        P("dp"),
        P("dp"),
        P("dp"),
        P(),
    )
    out_specs = (P("dp", "group"), P(None, None, "group"))
    return jax.shard_map(
        on_device, mesh=mesh, in_specs=in_specs, out_specs=out_specs, check_vma=False
    )
```

```python
import math

import jax
import jax.numpy as jnp
from jax import lax
from jax.experimental import pallas as pl
from jax.experimental.pallas import tpu as pltpu
from jax.sharding import PartitionSpec as P

BLK = 128
HOPS = 3
NZ, NY, NC = 8, 4, 2
NX = 4
NB = 4
SLOTS = NZ * NY * NB
EDGES = 256
UNROLL = 8
CHUNKS = 8
ITEMS = 264
HALF = 64
REST = BLK - HALF

bf16 = jnp.bfloat16
f32 = jnp.float32
MB = 1 << 20


def index_of(z, y, c):
    return ((z % NZ) * NY + (y % NY)) * NC + c


def shift(dz=0, dy=0, dc=0):
    return [
        (index_of(z, y, c), index_of(z + dz, y + dy, c ^ dc))
        for z in range(NZ)
        for y in range(NY)
        for c in range(NC)
    ]


Y_GROUPS = [[index_of(z, y, c) for y in range(NY)] for z in range(NZ) for c in range(NC)]
Z_GROUPS = [[index_of(z, y, c) for z in range(NZ)] for y in range(NY) for c in range(NC)]


YZ_GROUPS = [[index_of(z, y, c) for z in range(NZ) for y in range(NY)] for c in range(NC)]
PAIR = (2, NY // 2, NB, REST, BLK)
SUM_Y_COST = 1
SUMS = 512 // (NZ * NY)
ROWS = NB * HALF + 2 * SUMS
STIE = 4


def cost(us):
    return pl.CostEstimate(flops=0, bytes_accessed=int(us * 3_300_000), transcendentals=0)


def silu_slope(value):
    sigma = jax.nn.sigmoid(value)
    return sigma * (1.0 + value * (1.0 - sigma))


def vmem():
    return pl.BlockSpec(memory_space=pltpu.VMEM)


def params(limit):
    return pltpu.CompilerParams(vmem_limit_bytes=limit)


def factor_kernel(member, x_ref, w_ref, d_ref):
    for r in range(NB):
        z = jnp.dot(x_ref[0, r * BLK : (r + 1) * BLK, :], w_ref[0], preferred_element_type=f32)
        d_ref[r] = silu_slope(z.T)


def factors(member, saved, weights, hop):
    return pl.pallas_call(
        factor_kernel,
        out_shape=jax.ShapeDtypeStruct((NB, BLK, BLK), f32),
        grid_spec=pltpu.PrefetchScalarGridSpec(
            num_scalar_prefetch=1,
            grid=(1,),
            in_specs=[
                pl.BlockSpec((1, 512, 512), lambda i, m: (hop, 0, 0)),
                pl.BlockSpec((1, 512, BLK), lambda i, m: (hop, 0, m[0])),
            ],
            out_specs=pl.BlockSpec((NB, BLK, BLK), lambda i, m: (0, 0, 0)),
        ),
        compiler_params=params(60 * MB),
        name="factors",
    )(member, saved, weights)


def first_kernel(member, x_ref, w_ref, cot_ref, grad_ref, slope_ref):
    for r in range(NB):
        rows = slice(r * BLK, (r + 1) * BLK)
        z = jnp.dot(x_ref[0, rows, :], w_ref[0], preferred_element_type=f32)
        grad = cot_ref[rows, :].astype(f32).T
        grad_ref[r] = grad
        slope_ref[r] = (grad * silu_slope(z.T)).astype(bf16)


def first_slopes(member, saved, weights, cotangent):
    hop = HOPS - 1
    whole = pl.BlockSpec((NB, BLK, BLK), lambda i, m: (0, 0, 0))
    return pl.pallas_call(
        first_kernel,
        out_shape=(
            jax.ShapeDtypeStruct((NB, BLK, BLK), f32),
            jax.ShapeDtypeStruct((NB, BLK, BLK), bf16),
        ),
        grid_spec=pltpu.PrefetchScalarGridSpec(
            num_scalar_prefetch=1,
            grid=(1,),
            in_specs=[
                pl.BlockSpec((1, 512, 512), lambda i, m: (hop, 0, 0)),
                pl.BlockSpec((1, 512, BLK), lambda i, m: (hop, 0, m[0])),
                pl.BlockSpec((512, BLK), lambda i, m: (0, 0)),
            ],
            out_specs=(whole, whole),
        ),
        compiler_params=params(60 * MB),
        name="first_slopes",
    )(member, saved, weights, cotangent)


def upstream_kernel(member, w_ref, s0, s1, s2, s3, u_ref):
    me = member[0]
    parts = []
    for d in range(NX):
        start = pl.multiple_of(lax.rem(me - d + NX, NX) * BLK, BLK)
        parts.append(w_ref[:, pl.ds(start, BLK)])
    lhs = jnp.concatenate(parts, axis=1)
    for r in range(NB):
        rhs = jnp.concatenate([s[r] for s in (s0, s1, s2, s3)], axis=0)
        u_ref[r] = jnp.dot(lhs, rhs, preferred_element_type=f32).astype(bf16)


def upstream_of(member, rows, pieces):
    whole = pl.BlockSpec((NB, BLK, BLK), lambda i, m: (0, 0, 0))
    return pl.pallas_call(
        upstream_kernel,
        out_shape=jax.ShapeDtypeStruct((NB, BLK, BLK), bf16),
        grid_spec=pltpu.PrefetchScalarGridSpec(
            num_scalar_prefetch=1,
            grid=(1,),
            in_specs=[pl.BlockSpec((BLK, 512), lambda i, m: (0, 0))] + [whole] * NX,
            out_specs=whole,
        ),
        compiler_params=params(16 * MB),
        name="upstream",
    )(member, rows, *pieces)


def split(x):
    high = x.astype(bf16)
    return high, (x - high.astype(f32)).astype(bf16)


def joined(x):
    return x[:SUMS].astype(f32) + x[SUMS:].astype(f32)


def weight_kernel(x_ref, s_ref, out_ref, *, scale):
    lhs = jnp.concatenate([s_ref[r] for r in range(NB)], axis=1)
    part = jnp.dot(lhs, x_ref[0], preferred_element_type=f32).T * scale
    high, low = split(part)
    for z in range(NZ):
        for y in range(NY):
            start = (z * NY + y) * SUMS
            out_ref[y, z, :SUMS] = high[start : start + SUMS]
            out_ref[y, z, SUMS:] = low[start : start + SUMS]


def weight_part(saved, slopes, hop, scale):
    shape = (NY, NZ, 2 * SUMS, BLK)
    return pl.pallas_call(
        lambda *refs: weight_kernel(*refs, scale=scale),
        out_shape=jax.ShapeDtypeStruct(shape, bf16),
        grid=(1,),
        in_specs=[
            pl.BlockSpec((1, 512, 512), lambda i: (hop, 0, 0)),
            pl.BlockSpec((NB, BLK, BLK), lambda i: (0, 0, 0)),
        ],
        out_specs=pl.BlockSpec(shape, lambda i: (0, 0, 0, 0)),
        compiler_params=params(60 * MB),
        cost_estimate=cost(1),
        name="weight_part",
    )(saved, slopes)


def spread_kernel(a_ref, b_ref, out_ref):
    total = (a_ref[...] + b_ref[...]).astype(bf16)
    for i in range(NZ * NY):
        out_ref[i] = total


def spread(mine):
    theirs = lax.ppermute(mine, "dp", shift(dc=1))
    shape = (NZ * NY,) + mine.shape
    return pl.pallas_call(
        spread_kernel,
        out_shape=jax.ShapeDtypeStruct(shape, bf16),
        grid=(1,),
        in_specs=[pl.BlockSpec(mine.shape, lambda i: (0, 0))] * 2,
        out_specs=pl.BlockSpec(shape, lambda i: (0, 0, 0)),
        compiler_params=params(60 * MB),
        cost_estimate=cost(0.5),
        name="spread",
    )(mine, theirs)


def collect(copies):
    whole = lax.all_to_all(copies, "dp", 0, 0, axis_index_groups=YZ_GROUPS, tiled=True)
    whole = whole.reshape(NZ * NY, HOPS, SUMS, BLK).transpose(1, 0, 2, 3)
    return whole.reshape(HOPS, 512, BLK).astype(f32)


def message_kernel(table, own_ref, sib_ref, a_own, a_sib, weight_ref, out_a, *rest):
    out_b = rest[:NZ]
    edges, acc, up, stage, stage_b, sems, out_sems, out_b_sems = rest[NZ:]
    many = EDGES // 2 // CHUNKS
    copies = [
        pltpu.make_async_copy(
            source.at[pl.ds(i * many, many)],
            edges.at[pl.ds(side * (EDGES // 2) + i * many, many)],
            sems.at[side * CHUNKS + i],
        )
        for side, source in enumerate((a_own, a_sib))
        for i in range(CHUNKS)
    ]
    for copy in copies:
        copy.start()
    weight_copy = pltpu.make_async_copy(
        weight_ref, out_a.at[:, :, pl.ds(NB * HALF, 2 * SUMS)], sems.at[2 * CHUNKS]
    )
    weight_copy.start()
    up[0:NB] = own_ref[...]
    up[NB : 2 * NB] = sib_ref[...]
    up[2 * NB] = jnp.zeros((BLK, BLK), bf16)

    @pl.loop(0, SLOTS // 4)
    def _(i):
        acc[pl.ds(i * 4, 4)] = jnp.zeros((4, BLK, BLK), f32)

    n_items, n_own = table[5 * ITEMS], table[5 * ITEMS + 3]

    def add_items(i):
        sums = []
        for j in range(UNROLL):
            at = i * UNROLL + j
            lhs = jnp.concatenate([up[table[3 * ITEMS + at]], up[table[4 * ITEMS + at]]], axis=1)
            rhs = jnp.concatenate([edges[table[ITEMS + at]], edges[table[2 * ITEMS + at]]], axis=0)
            sums.append(jnp.dot(lhs, rhs, preferred_element_type=f32))
        for j in range(UNROLL):
            slot = table[i * UNROLL + j]
            acc[slot] = acc[slot] + sums[j]

    early = n_own // UNROLL
    for copy in copies[:CHUNKS]:
        copy.wait()
    pl.loop(0, early)(add_items)
    for copy in copies[CHUNKS:]:
        copy.wait()
    pl.loop(early, (n_items + UNROLL - 1) // UNROLL)(add_items)

    z, y = table[5 * ITEMS + 1], table[5 * ITEMS + 2]
    sends = []
    for dz in range(NZ):
        for dy in range(NY):
            place = dz * 2 + dy // 2
            for b in range(NB):
                total = acc[(dz * NY + dy) * NB + b].astype(bf16)
                stage[dz, dy, b * HALF : (b + 1) * HALF] = total[:HALF]
                stage_b[(place + 1) // 2 % NZ, (place + 1) % 2, dy % 2, b] = total[HALF:]
            send = pltpu.make_async_copy(
                stage.at[dz, dy],
                out_a.at[lax.rem(y + dy, NY), lax.rem(z + dz, NZ), pl.ds(0, NB * HALF)],
                out_sems.at[dz * NY + dy],
            )
            send.start()
            sends.append(send)
        ready = [dz] if dz else []
        if dz == NZ - 1:
            ready.append(0)
        for pair in ready:
            send = pltpu.make_async_copy(stage_b.at[pair], out_b[pair], out_b_sems.at[pair])
            send.start()
            sends.append(send)
    for send in sends:
        send.wait()
    weight_copy.wait()


def messages_of(table, own, sibling, a_own, a_sib, weight):
    hbm = pl.BlockSpec(memory_space=pltpu.HBM)
    return pl.pallas_call(
        message_kernel,
        out_shape=(jax.ShapeDtypeStruct((NY, NZ, ROWS, BLK), bf16),)
        + (jax.ShapeDtypeStruct(PAIR, bf16),) * NZ,
        in_specs=[pl.BlockSpec(memory_space=pltpu.SMEM), vmem(), vmem(), hbm, hbm, vmem()],
        out_specs=(hbm,) * (NZ + 1),
        scratch_shapes=[
            pltpu.VMEM((EDGES, BLK, BLK), bf16),
            pltpu.VMEM((SLOTS + 1, BLK, BLK), f32),
            pltpu.VMEM((2 * NB + 1, BLK, BLK), bf16),
            pltpu.VMEM((NZ, NY, NB * HALF, BLK), bf16),
            pltpu.VMEM((NZ,) + PAIR, bf16),
            pltpu.SemaphoreType.DMA((2 * CHUNKS + 1,)),
            pltpu.SemaphoreType.DMA((NZ * NY,)),
            pltpu.SemaphoreType.DMA((NZ,)),
        ],
        compiler_params=params(60 * MB),
        cost_estimate=cost(6),
        name="messages",
    )(table, own, sibling, a_own, a_sib, weight)


def arrivals(from_z, from_y, r):
    rows = slice(r * HALF, (r + 1) * HALF)
    first = from_z[0, rows].astype(f32)
    for i in range(1, NZ):
        first += from_z[i, rows].astype(f32)
    second = from_y[0][r].astype(f32)
    for part in from_y[1:]:
        second += part[r].astype(f32)
    return jnp.concatenate([first, second], axis=0)


def weight_sums(from_z):
    total = joined(from_z[0, NB * HALF :])
    for i in range(1, NZ):
        total += joined(from_z[i, NB * HALF :])
    return total


def update_kernel(from_z, *refs):
    from_y, (grad_ref, d_ref, new_ref, slope_ref, sums_ref) = refs[:NY], refs[NY:]
    for r in range(NB):
        grad = grad_ref[r] + arrivals(from_z, from_y, r)
        new_ref[r] = grad
        slope_ref[r] = (grad * d_ref[r]).astype(bf16)
    sums_ref[...] = weight_sums(from_z)


def update(from_z, from_y, grad, factor):
    return pl.pallas_call(
        update_kernel,
        out_shape=(
            jax.ShapeDtypeStruct((NB, BLK, BLK), f32),
            jax.ShapeDtypeStruct((NB, BLK, BLK), bf16),
            jax.ShapeDtypeStruct((SUMS, BLK), f32),
        ),
        in_specs=[vmem()] * (NY + 3),
        out_specs=(vmem(),) * 3,
        compiler_params=params(16 * MB),
        cost_estimate=cost(1),
        name="update",
    )(from_z, *from_y, grad, factor)


def last_kernel(from_z, *refs):
    from_y, (grad_ref, out_ref) = refs[:NY], refs[NY:]
    for r in range(NB):
        grad = grad_ref[r] + arrivals(from_z, from_y, r)
        out_ref[r * BLK : (r + 1) * BLK, :] = grad.T.astype(bf16)


def last_update(from_z, from_y, grad):
    return pl.pallas_call(
        last_kernel,
        out_shape=jax.ShapeDtypeStruct((NB * BLK, BLK), bf16),
        in_specs=[vmem()] * (NY + 2),
        out_specs=vmem(),
        compiler_params=params(16 * MB),
        cost_estimate=cost(1),
        name="last_update",
    )(from_z, *from_y, grad)


def last_sums_kernel(from_z, out_ref):
    out_ref[...] = weight_sums(from_z)


def last_sums(from_z):
    return pl.pallas_call(
        last_sums_kernel,
        out_shape=jax.ShapeDtypeStruct((SUMS, BLK), f32),
        grid=(1,),
        in_specs=[pl.BlockSpec((NZ, ROWS, BLK), lambda i: (0, 0, 0))],
        out_specs=pl.BlockSpec((SUMS, BLK), lambda i: (0, 0)),
        compiler_params=params(16 * MB),
        cost_estimate=cost(0.5),
        name="last_sums",
    )(from_z)


def plus(a, b):
    return (a.astype(f32) + b.astype(f32)).astype(bf16)


def fetch(held, sems, *sources):
    copies = [
        pltpu.make_async_copy(q, held.at[i], sems.at[i]) for i, q in enumerate(sources)
    ]
    for copy in copies:
        copy.start()
    for copy in copies:
        copy.wait()


def step_kernel(q_up, q_down, got_up, got_down, up, down, held, sems):
    fetch(held, sems, q_up, q_down)
    up[...] = plus(held[0], got_up[...])
    down[...] = plus(held[1], got_down[...])


def final_kernel(q_up, q_down, got_up, got_down, up, down, keep, held, sems):
    fetch(held, sems, q_up, q_down)
    up[...] = plus(held[0, 1], got_up[1])
    down[...] = plus(held[1, 0], got_down[0])
    keep[0] = held[1, 1].astype(f32) + got_down[1].astype(f32)
    keep[1] = held[0, 0].astype(f32) + got_up[0].astype(f32)


def step(q_up, q_down, got_up, got_down, final):
    hbm = pl.BlockSpec(memory_space=pltpu.HBM)
    sent = jax.ShapeDtypeStruct(PAIR[1:] if final else PAIR, bf16)
    kept = (jax.ShapeDtypeStruct(PAIR, f32),) if final else ()
    return pl.pallas_call(
        final_kernel if final else step_kernel,
        out_shape=(sent, sent) + kept,
        in_specs=[hbm, hbm, vmem(), vmem()],
        out_specs=(vmem(),) * (3 if final else 2),
        scratch_shapes=[pltpu.VMEM((2,) + PAIR, bf16), pltpu.SemaphoreType.DMA((2,))],
        compiler_params=params(4 * MB),
        cost_estimate=cost(0.5),
        name="final_step" if final else "step",
    )(q_up, q_down, got_up, got_down)


def ring_end_kernel(keep, last_up, last_down, *out):
    for i, last in enumerate((last_up, last_down)):
        total = keep[i] + last[...].astype(f32)
        for j in range(NY // 2):
            at = out[i * (NY // 2) + j]
            at[...] = total[j].astype(at.dtype)


def ring_end(keep, last_up, last_down):
    shape = (NB, REST, BLK)
    return pl.pallas_call(
        ring_end_kernel,
        out_shape=(jax.ShapeDtypeStruct(shape, f32),)
        + (jax.ShapeDtypeStruct(shape, bf16),) * (NY - 1),
        in_specs=[vmem()] * 3,
        out_specs=(vmem(),) * NY,
        compiler_params=params(4 * MB),
        cost_estimate=cost(0.5),
        name="ring_end",
    )(keep, last_up, last_down)


def ring(q, tie):
    ahead, back = shift(dz=1), shift(dz=-1)
    up, down = q[NZ // 2], q[NZ // 2 + 1]
    keep = None
    for k in range(1, NZ // 2):
        got_up = lax.ppermute(up, "dp", ahead)
        got_down = lax.ppermute(down, "dp", back)
        got_up, got_down = tie(k, got_up, got_down)
        args = (q[NZ // 2 - k], q[(NZ // 2 + 1 + k) % NZ], got_up, got_down)
        up, down, *keep = step(*args, k == NZ // 2 - 1)
    last_up = lax.ppermute(up, "dp", ahead)
    last_down = lax.ppermute(down, "dp", back)
    last_up, last_down = tie(NZ // 2, last_up, last_down)
    return ring_end(*keep, last_up, last_down)


def sum_y_kernel(x_ref, out_ref, held, made, sems, out_sems):
    copies, sends = [], []
    for i in range(NZ // 2):
        two = pl.ds(2 * i, 2)
        copies.append(pltpu.make_async_copy(x_ref.at[:, two], held.at[:, two], sems.at[i]))
        sends.append(pltpu.make_async_copy(made.at[two], out_ref.at[two], out_sems.at[i]))
    for copy in copies:
        copy.start()
    for i in range(NZ // 2):
        two = slice(2 * i, 2 * i + 2)
        copies[i].wait()
        total = held[0, two].astype(f32)
        for j in range(1, NY):
            total += held[j, two].astype(f32)
        made[two] = total.astype(bf16)
        for j in (2 * i, 2 * i + 1):
            part = joined(held[0, j, NB * HALF :])
            for k in range(1, NY):
                part += joined(held[k, j, NB * HALF :])
            high, low = split(part)
            made[j, NB * HALF : NB * HALF + SUMS] = high
            made[j, NB * HALF + SUMS :] = low
        sends[i].start()
    for send in sends:
        send.wait()


def sum_y(x):
    hbm = pl.BlockSpec(memory_space=pltpu.HBM)
    return pl.pallas_call(
        sum_y_kernel,
        out_shape=jax.ShapeDtypeStruct(x.shape[1:], bf16),
        in_specs=[hbm],
        out_specs=hbm,
        scratch_shapes=[
            pltpu.VMEM(x.shape, bf16),
            pltpu.VMEM(x.shape[1:], bf16),
            pltpu.SemaphoreType.DMA((NZ // 2,)),
            pltpu.SemaphoreType.DMA((NZ // 2,)),
        ],
        compiler_params=params(60 * MB),
        cost_estimate=cost(SUM_Y_COST),
        name="sum_y",
    )(x)


def exchange(out_a, out_b):
    by_y = lax.all_to_all(out_a, "dp", 0, 0, axis_index_groups=Y_GROUPS, tiled=True)
    made = {"sums": sum_y(by_y)}

    def tie(k, up, down):
        if k == STIE:
            up, down, made["sums"] = lax.optimization_barrier((up, down, made["sums"]))
        return up, down

    own, *others = ring(out_b, tie)
    from_z = lax.all_to_all(made["sums"], "dp", 0, 0, axis_index_groups=Z_GROUPS, tiled=True)
    from_y = [own] + [lax.ppermute(x, "dp", shift(dy=d + 1)) for d, x in enumerate(others)]
    return from_z, from_y


def routing(edge_rows, edge_cols, edge_counts, block_owner, z, y, c):
    live = jnp.arange(EDGES // 2, dtype=jnp.int32) < edge_counts[0]
    code = jnp.where(live, block_owner[edge_cols], -1)
    mine = jnp.stack([code, edge_rows])
    theirs = lax.ppermute(mine, "dp", shift(dc=1))
    code = jnp.concatenate([mine[0], theirs[0]])
    rows = jnp.concatenate([mine[1], theirs[1] + NB])
    dev = code // NB
    used = (code >= 0) & (dev % NC == c)
    y_to, z_to = (dev // NC) % NY, dev // (NC * NY)
    slot = jnp.where(used, ((z_to - z + NZ) % NZ * NY + (y_to - y + NY) % NY) * NB + code % NB, SLOTS)
    ids = jnp.arange(EDGES, dtype=jnp.int32)
    key = jnp.where(used, slot + SLOTS * (ids // (EDGES // 2)), 2 * SLOTS)
    keys = jnp.arange(2 * SLOTS, dtype=jnp.int32)
    same = (key[:, None] == key[None, :]) & (ids[None, :] < ids[:, None])
    rank = jnp.sum(same.astype(jnp.int32), axis=1)
    hit = (key[:, None] == keys[None, :]).astype(jnp.int32)
    pairs = (jnp.sum(hit, axis=0) + 1) // 2
    base = jnp.sum(jnp.where(keys[None, :] < keys[:, None], pairs[None, :], 0), axis=1)
    item = jnp.where(used, jnp.sum(hit * base[None, :], axis=1) + rank // 2, -1)
    side = rank % 2
    place = jnp.arange(ITEMS, dtype=jnp.int32)
    at = [
        (place[:, None] == item[None, :]) & (side[None, :] == s) for s in range(2)
    ]

    def pick(mask, values, default):
        return jnp.sum(jnp.where(mask, values[None, :] - default, 0), axis=1) + default

    return jnp.concatenate(
        [
            pick(at[0], slot, SLOTS),
            pick(at[0], ids, 0),
            pick(at[1], ids, 0),
            pick(at[0], rows, 2 * NB),
            pick(at[1], rows, 2 * NB),
            jnp.stack([jnp.sum(pairs), z, y, jnp.sum(pairs[:SLOTS])]),
        ]
    ).astype(jnp.int32)


def on_device(
    cotangent, saved_inputs, weights, edge_values, edge_rows, edge_cols, edge_counts, block_owner
):
    scale = 1.0 / math.sqrt(saved_inputs.shape[1] * lax.axis_size("dp"))
    dp = lax.axis_index("dp")
    z, y, c = dp // (NY * NC), dp // NC % NY, dp % NC
    group = lax.axis_index("group")
    member = jnp.full((1,), group, jnp.int32)

    edges_sib = lax.ppermute(edge_values, "dp", shift(dc=1))
    table = routing(edge_rows, edge_cols, edge_counts, block_owner, z, y, c)
    grad, slopes = first_slopes(member, saved_inputs, weights, cotangent)
    factor = [factors(member, saved_inputs, weights, h) for h in range(HOPS - 1)]

    my_rows = [
        lax.dynamic_slice(weights, (h, group * BLK, 0), (1, BLK, 512))[0] for h in range(HOPS)
    ]
    sums = [None] * HOPS
    for hop in reversed(range(HOPS)):
        pieces = [slopes] + [
            lax.ppermute(slopes, "group", [(i, (i + d) % NX) for i in range(NX)])
            for d in range(1, NX)
        ]
        weight = weight_part(saved_inputs, slopes, hop, scale)
        own = upstream_of(member, my_rows[hop], pieces)
        sibling = lax.ppermute(own, "dp", shift(dc=1))
        out_a, *out_b = messages_of(table, own, sibling, edge_values, edges_sib, weight)
        from_z, from_y = exchange(out_a, out_b)
        if hop:
            grad, slopes, sums[hop] = update(from_z, from_y, grad, factor[hop - 1])
    result = last_update(from_z, from_y, grad)
    sums[0] = last_sums(from_z)
    return result, collect(spread(jnp.concatenate(sums, axis=0)))


def solution(mesh):
    in_specs = (
        P("dp", "group"),
        P(None, "dp", None),
        P(),
        P("dp", None, None),
        P("dp"),
        P("dp"),
        P("dp"),
        P(),
    )
    out_specs = (P("dp", "group"), P(None, None, "group"))
    return jax.shard_map(
        on_device, mesh=mesh, in_specs=in_specs, out_specs=out_specs, check_vma=False
    )
```

```python
import math

import jax
import jax.numpy as jnp
from jax import lax
from jax.experimental import pallas as pl
from jax.experimental.pallas import tpu as pltpu
from jax.sharding import PartitionSpec as P

BLK = 128
HOPS = 3
NZ, NY, NC = 8, 4, 2
NX = 4
NB = 4
SLOTS = NZ * NY * NB
EDGES = 256
UNROLL = 8
CHUNKS = 8
ITEMS = 264
HALF = 64
REST = BLK - HALF

bf16 = jnp.bfloat16
f32 = jnp.float32
MB = 1 << 20


def index_of(z, y, c):
    return ((z % NZ) * NY + (y % NY)) * NC + c


def shift(dz=0, dy=0, dc=0):
    return [
        (index_of(z, y, c), index_of(z + dz, y + dy, c ^ dc))
        for z in range(NZ)
        for y in range(NY)
        for c in range(NC)
    ]


Y_GROUPS = [[index_of(z, y, c) for y in range(NY)] for z in range(NZ) for c in range(NC)]
Z_GROUPS = [[index_of(z, y, c) for z in range(NZ)] for y in range(NY) for c in range(NC)]


YZ_GROUPS = [[index_of(z, y, c) for z in range(NZ) for y in range(NY)] for c in range(NC)]
PAIR = (2, NY // 2, NB, REST, BLK)
SUM_Y_COST = 1
SUMS = 512 // (NZ * NY)
ROWS = NB * HALF + 2 * SUMS
STIE = 4


def cost(us):
    return pl.CostEstimate(flops=0, bytes_accessed=int(us * 3_300_000), transcendentals=0)


def silu_slope(value):
    sigma = jax.nn.sigmoid(value)
    return sigma * (1.0 + value * (1.0 - sigma))


def vmem():
    return pl.BlockSpec(memory_space=pltpu.VMEM)


def params(limit):
    return pltpu.CompilerParams(vmem_limit_bytes=limit)


def factor_kernel(member, x_ref, w_ref, d_ref):
    for r in range(NB):
        z = jnp.dot(x_ref[0, r * BLK : (r + 1) * BLK, :], w_ref[0], preferred_element_type=f32)
        d_ref[r] = silu_slope(z.T)


def factors(member, saved, weights, hop):
    return pl.pallas_call(
        factor_kernel,
        out_shape=jax.ShapeDtypeStruct((NB, BLK, BLK), f32),
        grid_spec=pltpu.PrefetchScalarGridSpec(
            num_scalar_prefetch=1,
            grid=(1,),
            in_specs=[
                pl.BlockSpec((1, 512, 512), lambda i, m: (hop, 0, 0)),
                pl.BlockSpec((1, 512, BLK), lambda i, m: (hop, 0, m[0])),
            ],
            out_specs=pl.BlockSpec((NB, BLK, BLK), lambda i, m: (0, 0, 0)),
        ),
        compiler_params=params(60 * MB),
        name="factors",
    )(member, saved, weights)


def first_kernel(member, x_ref, w_ref, cot_ref, grad_ref, slope_ref):
    for r in range(NB):
        rows = slice(r * BLK, (r + 1) * BLK)
        z = jnp.dot(x_ref[0, rows, :], w_ref[0], preferred_element_type=f32)
        grad = cot_ref[rows, :].astype(f32).T
        grad_ref[r] = grad
        slope_ref[r] = (grad * silu_slope(z.T)).astype(bf16)


def first_slopes(member, saved, weights, cotangent):
    hop = HOPS - 1
    whole = pl.BlockSpec((NB, BLK, BLK), lambda i, m: (0, 0, 0))
    return pl.pallas_call(
        first_kernel,
        out_shape=(
            jax.ShapeDtypeStruct((NB, BLK, BLK), f32),
            jax.ShapeDtypeStruct((NB, BLK, BLK), bf16),
        ),
        grid_spec=pltpu.PrefetchScalarGridSpec(
            num_scalar_prefetch=1,
            grid=(1,),
            in_specs=[
                pl.BlockSpec((1, 512, 512), lambda i, m: (hop, 0, 0)),
                pl.BlockSpec((1, 512, BLK), lambda i, m: (hop, 0, m[0])),
                pl.BlockSpec((512, BLK), lambda i, m: (0, 0)),
            ],
            out_specs=(whole, whole),
        ),
        compiler_params=params(60 * MB),
        name="first_slopes",
    )(member, saved, weights, cotangent)


def upstream_kernel(member, w_ref, s0, s1, s2, s3, u_ref):
    me = member[0]
    parts = []
    for d in range(NX):
        start = pl.multiple_of(lax.rem(me - d + NX, NX) * BLK, BLK)
        parts.append(w_ref[:, pl.ds(start, BLK)])
    lhs = jnp.concatenate(parts, axis=1)
    for r in range(NB):
        rhs = jnp.concatenate([s[r] for s in (s0, s1, s2, s3)], axis=0)
        u_ref[r] = jnp.dot(lhs, rhs, preferred_element_type=f32).astype(bf16)


def upstream_of(member, rows, pieces):
    whole = pl.BlockSpec((NB, BLK, BLK), lambda i, m: (0, 0, 0))
    return pl.pallas_call(
        upstream_kernel,
        out_shape=jax.ShapeDtypeStruct((NB, BLK, BLK), bf16),
        grid_spec=pltpu.PrefetchScalarGridSpec(
            num_scalar_prefetch=1,
            grid=(1,),
            in_specs=[pl.BlockSpec((BLK, 512), lambda i, m: (0, 0))] + [whole] * NX,
            out_specs=whole,
        ),
        compiler_params=params(16 * MB),
        name="upstream",
    )(member, rows, *pieces)


def split(x):
    high = x.astype(bf16)
    return high, (x - high.astype(f32)).astype(bf16)


def joined(x):
    return x[:SUMS].astype(f32) + x[SUMS:].astype(f32)


def weight_kernel(x_ref, s_ref, out_ref, *, scale):
    lhs = jnp.concatenate([s_ref[r] for r in range(NB)], axis=1)
    part = jnp.dot(lhs, x_ref[0], preferred_element_type=f32).T * scale
    high, low = split(part)
    for z in range(NZ):
        for y in range(NY):
            start = (z * NY + y) * SUMS
            out_ref[y, z, :SUMS] = high[start : start + SUMS]
            out_ref[y, z, SUMS:] = low[start : start + SUMS]


def weight_part(saved, slopes, hop, scale):
    shape = (NY, NZ, 2 * SUMS, BLK)
    return pl.pallas_call(
        lambda *refs: weight_kernel(*refs, scale=scale),
        out_shape=jax.ShapeDtypeStruct(shape, bf16),
        grid=(1,),
        in_specs=[
            pl.BlockSpec((1, 512, 512), lambda i: (hop, 0, 0)),
            pl.BlockSpec((NB, BLK, BLK), lambda i: (0, 0, 0)),
        ],
        out_specs=pl.BlockSpec(shape, lambda i: (0, 0, 0, 0)),
        compiler_params=params(60 * MB),
        cost_estimate=cost(4),
        name="weight_part",
    )(saved, slopes)


def spread_kernel(a_ref, b_ref, out_ref):
    total = (a_ref[...] + b_ref[...]).astype(bf16)
    for i in range(NZ * NY):
        out_ref[i] = total


def spread(mine):
    theirs = lax.ppermute(mine, "dp", shift(dc=1))
    shape = (NZ * NY,) + mine.shape
    return pl.pallas_call(
        spread_kernel,
        out_shape=jax.ShapeDtypeStruct(shape, bf16),
        grid=(1,),
        in_specs=[pl.BlockSpec(mine.shape, lambda i: (0, 0))] * 2,
        out_specs=pl.BlockSpec(shape, lambda i: (0, 0, 0)),
        compiler_params=params(8 * MB),
        cost_estimate=cost(0.5),
        name="spread",
    )(mine, theirs)


def collect(copies):
    whole = lax.all_to_all(copies, "dp", 0, 0, axis_index_groups=YZ_GROUPS, tiled=True)
    whole = whole.reshape(NZ * NY, HOPS, SUMS, BLK).transpose(1, 0, 2, 3)
    return whole.reshape(HOPS, 512, BLK).astype(f32)


def message_kernel(table, own_ref, sib_ref, a_own, a_sib, weight_ref, out_a, *rest):
    out_b = rest[:NZ]
    edges, acc, up, stage, stage_b, sems, out_sems, out_b_sems = rest[NZ:]
    many = EDGES // 2 // CHUNKS
    copies = [
        pltpu.make_async_copy(
            source.at[pl.ds(i * many, many)],
            edges.at[pl.ds(side * (EDGES // 2) + i * many, many)],
            sems.at[side * CHUNKS + i],
        )
        for side, source in enumerate((a_own, a_sib))
        for i in range(CHUNKS)
    ]
    for copy in copies:
        copy.start()
    weight_copy = pltpu.make_async_copy(
        weight_ref, out_a.at[:, :, pl.ds(NB * HALF, 2 * SUMS)], sems.at[2 * CHUNKS]
    )
    weight_copy.start()
    up[0:NB] = own_ref[...]
    up[NB : 2 * NB] = sib_ref[...]
    up[2 * NB] = jnp.zeros((BLK, BLK), bf16)

    @pl.loop(0, SLOTS // 4)
    def _(i):
        acc[pl.ds(i * 4, 4)] = jnp.zeros((4, BLK, BLK), f32)

    n_items, n_own = table[5 * ITEMS], table[5 * ITEMS + 3]

    def add_items(i):
        sums = []
        for j in range(UNROLL):
            at = i * UNROLL + j
            lhs = jnp.concatenate([up[table[3 * ITEMS + at]], up[table[4 * ITEMS + at]]], axis=1)
            rhs = jnp.concatenate([edges[table[ITEMS + at]], edges[table[2 * ITEMS + at]]], axis=0)
            sums.append(jnp.dot(lhs, rhs, preferred_element_type=f32))
        for j in range(UNROLL):
            slot = table[i * UNROLL + j]
            acc[slot] = acc[slot] + sums[j]

    early = n_own // UNROLL
    for copy in copies[:CHUNKS]:
        copy.wait()
    pl.loop(0, early)(add_items)
    for copy in copies[CHUNKS:]:
        copy.wait()
    pl.loop(early, (n_items + UNROLL - 1) // UNROLL)(add_items)

    z, y = table[5 * ITEMS + 1], table[5 * ITEMS + 2]
    sends = []
    for dz in range(NZ):
        for dy in range(NY):
            place = dz * 2 + dy // 2
            for b in range(NB):
                total = acc[(dz * NY + dy) * NB + b].astype(bf16)
                stage[dz, dy, b * HALF : (b + 1) * HALF] = total[:HALF]
                stage_b[(place + 1) // 2 % NZ, (place + 1) % 2, dy % 2, b] = total[HALF:]
            send = pltpu.make_async_copy(
                stage.at[dz, dy],
                out_a.at[lax.rem(y + dy, NY), lax.rem(z + dz, NZ), pl.ds(0, NB * HALF)],
                out_sems.at[dz * NY + dy],
            )
            send.start()
            sends.append(send)
        ready = [dz] if dz else []
        if dz == NZ - 1:
            ready.append(0)
        for pair in ready:
            send = pltpu.make_async_copy(stage_b.at[pair], out_b[pair], out_b_sems.at[pair])
            send.start()
            sends.append(send)
    for send in sends:
        send.wait()
    weight_copy.wait()


def messages_of(table, own, sibling, a_own, a_sib, weight):
    hbm = pl.BlockSpec(memory_space=pltpu.HBM)
    return pl.pallas_call(
        message_kernel,
        out_shape=(jax.ShapeDtypeStruct((NY, NZ, ROWS, BLK), bf16),)
        + (jax.ShapeDtypeStruct(PAIR, bf16),) * NZ,
        in_specs=[pl.BlockSpec(memory_space=pltpu.SMEM), vmem(), vmem(), hbm, hbm, vmem()],
        out_specs=(hbm,) * (NZ + 1),
        scratch_shapes=[
            pltpu.VMEM((EDGES, BLK, BLK), bf16),
            pltpu.VMEM((SLOTS + 1, BLK, BLK), f32),
            pltpu.VMEM((2 * NB + 1, BLK, BLK), bf16),
            pltpu.VMEM((NZ, NY, NB * HALF, BLK), bf16),
            pltpu.VMEM((NZ,) + PAIR, bf16),
            pltpu.SemaphoreType.DMA((2 * CHUNKS + 1,)),
            pltpu.SemaphoreType.DMA((NZ * NY,)),
            pltpu.SemaphoreType.DMA((NZ,)),
        ],
        compiler_params=params(60 * MB),
        cost_estimate=cost(6),
        name="messages",
    )(table, own, sibling, a_own, a_sib, weight)


def arrivals(from_z, from_y, r):
    rows = slice(r * HALF, (r + 1) * HALF)
    first = from_z[0, rows].astype(f32)
    for i in range(1, NZ):
        first += from_z[i, rows].astype(f32)
    second = from_y[0][r].astype(f32)
    for part in from_y[1:]:
        second += part[r].astype(f32)
    return jnp.concatenate([first, second], axis=0)


def weight_sums(from_z):
    total = joined(from_z[0, NB * HALF :])
    for i in range(1, NZ):
        total += joined(from_z[i, NB * HALF :])
    return total


def update_kernel(from_z, *refs):
    from_y, (grad_ref, d_ref, new_ref, slope_ref, sums_ref) = refs[:NY], refs[NY:]
    for r in range(NB):
        grad = grad_ref[r] + arrivals(from_z, from_y, r)
        new_ref[r] = grad
        slope_ref[r] = (grad * d_ref[r]).astype(bf16)
    sums_ref[...] = weight_sums(from_z)


def update(from_z, from_y, grad, factor):
    return pl.pallas_call(
        update_kernel,
        out_shape=(
            jax.ShapeDtypeStruct((NB, BLK, BLK), f32),
            jax.ShapeDtypeStruct((NB, BLK, BLK), bf16),
            jax.ShapeDtypeStruct((SUMS, BLK), f32),
        ),
        in_specs=[vmem()] * (NY + 3),
        out_specs=(vmem(),) * 3,
        compiler_params=params(16 * MB),
        cost_estimate=cost(1),
        name="update",
    )(from_z, *from_y, grad, factor)


def last_kernel(from_z, *refs):
    from_y, (grad_ref, out_ref) = refs[:NY], refs[NY:]
    for r in range(NB):
        grad = grad_ref[r] + arrivals(from_z, from_y, r)
        out_ref[r * BLK : (r + 1) * BLK, :] = grad.T.astype(bf16)


def last_update(from_z, from_y, grad):
    return pl.pallas_call(
        last_kernel,
        out_shape=jax.ShapeDtypeStruct((NB * BLK, BLK), bf16),
        in_specs=[vmem()] * (NY + 2),
        out_specs=vmem(),
        compiler_params=params(16 * MB),
        cost_estimate=cost(1),
        name="last_update",
    )(from_z, *from_y, grad)


def last_sums_kernel(from_z, out_ref):
    out_ref[...] = weight_sums(from_z)


def last_sums(from_z):
    return pl.pallas_call(
        last_sums_kernel,
        out_shape=jax.ShapeDtypeStruct((SUMS, BLK), f32),
        grid=(1,),
        in_specs=[pl.BlockSpec((NZ, ROWS, BLK), lambda i: (0, 0, 0))],
        out_specs=pl.BlockSpec((SUMS, BLK), lambda i: (0, 0)),
        compiler_params=params(16 * MB),
        cost_estimate=cost(0.5),
        name="last_sums",
    )(from_z)


def plus(a, b):
    return (a.astype(f32) + b.astype(f32)).astype(bf16)


def fetch(held, sems, *sources):
    copies = [
        pltpu.make_async_copy(q, held.at[i], sems.at[i]) for i, q in enumerate(sources)
    ]
    for copy in copies:
        copy.start()
    for copy in copies:
        copy.wait()


def step_kernel(q_up, q_down, got_up, got_down, up, down, held, sems):
    fetch(held, sems, q_up, q_down)
    up[...] = plus(held[0], got_up[...])
    down[...] = plus(held[1], got_down[...])


def final_kernel(q_up, q_down, got_up, got_down, up, down, keep, held, sems):
    fetch(held, sems, q_up, q_down)
    up[...] = plus(held[0, 1], got_up[1])
    down[...] = plus(held[1, 0], got_down[0])
    keep[0] = held[1, 1].astype(f32) + got_down[1].astype(f32)
    keep[1] = held[0, 0].astype(f32) + got_up[0].astype(f32)


def step(q_up, q_down, got_up, got_down, final):
    hbm = pl.BlockSpec(memory_space=pltpu.HBM)
    sent = jax.ShapeDtypeStruct(PAIR[1:] if final else PAIR, bf16)
    kept = (jax.ShapeDtypeStruct(PAIR, f32),) if final else ()
    return pl.pallas_call(
        final_kernel if final else step_kernel,
        out_shape=(sent, sent) + kept,
        in_specs=[hbm, hbm, vmem(), vmem()],
        out_specs=(vmem(),) * (3 if final else 2),
        scratch_shapes=[pltpu.VMEM((2,) + PAIR, bf16), pltpu.SemaphoreType.DMA((2,))],
        compiler_params=params(4 * MB),
        cost_estimate=cost(0.5),
        name="final_step" if final else "step",
    )(q_up, q_down, got_up, got_down)


def ring_end_kernel(keep, last_up, last_down, *out):
    for i, last in enumerate((last_up, last_down)):
        total = keep[i] + last[...].astype(f32)
        for j in range(NY // 2):
            at = out[i * (NY // 2) + j]
            at[...] = total[j].astype(at.dtype)


def ring_end(keep, last_up, last_down):
    shape = (NB, REST, BLK)
    return pl.pallas_call(
        ring_end_kernel,
        out_shape=(jax.ShapeDtypeStruct(shape, f32),)
        + (jax.ShapeDtypeStruct(shape, bf16),) * (NY - 1),
        in_specs=[vmem()] * 3,
        out_specs=(vmem(),) * NY,
        compiler_params=params(4 * MB),
        cost_estimate=cost(0.5),
        name="ring_end",
    )(keep, last_up, last_down)


def ring(q, tie):
    ahead, back = shift(dz=1), shift(dz=-1)
    up, down = q[NZ // 2], q[NZ // 2 + 1]
    keep = None
    for k in range(1, NZ // 2):
        got_up = lax.ppermute(up, "dp", ahead)
        got_down = lax.ppermute(down, "dp", back)
        got_up, got_down = tie(k, got_up, got_down)
        args = (q[NZ // 2 - k], q[(NZ // 2 + 1 + k) % NZ], got_up, got_down)
        up, down, *keep = step(*args, k == NZ // 2 - 1)
    last_up = lax.ppermute(up, "dp", ahead)
    last_down = lax.ppermute(down, "dp", back)
    last_up, last_down = tie(NZ // 2, last_up, last_down)
    return ring_end(*keep, last_up, last_down)


def sum_y_kernel(x_ref, out_ref, held, made, sems, out_sems):
    copies, sends = [], []
    for i in range(NZ // 2):
        two = pl.ds(2 * i, 2)
        copies.append(pltpu.make_async_copy(x_ref.at[:, two], held.at[:, two], sems.at[i]))
        sends.append(pltpu.make_async_copy(made.at[two], out_ref.at[two], out_sems.at[i]))
    for copy in copies:
        copy.start()
    for i in range(NZ // 2):
        two = slice(2 * i, 2 * i + 2)
        copies[i].wait()
        total = held[0, two].astype(f32)
        for j in range(1, NY):
            total += held[j, two].astype(f32)
        made[two] = total.astype(bf16)
        for j in (2 * i, 2 * i + 1):
            part = joined(held[0, j, NB * HALF :])
            for k in range(1, NY):
                part += joined(held[k, j, NB * HALF :])
            high, low = split(part)
            made[j, NB * HALF : NB * HALF + SUMS] = high
            made[j, NB * HALF + SUMS :] = low
        sends[i].start()
    for send in sends:
        send.wait()


def sum_y(x):
    hbm = pl.BlockSpec(memory_space=pltpu.HBM)
    return pl.pallas_call(
        sum_y_kernel,
        out_shape=jax.ShapeDtypeStruct(x.shape[1:], bf16),
        in_specs=[hbm],
        out_specs=hbm,
        scratch_shapes=[
            pltpu.VMEM(x.shape, bf16),
            pltpu.VMEM(x.shape[1:], bf16),
            pltpu.SemaphoreType.DMA((NZ // 2,)),
            pltpu.SemaphoreType.DMA((NZ // 2,)),
        ],
        compiler_params=params(60 * MB),
        cost_estimate=cost(SUM_Y_COST),
        name="sum_y",
    )(x)


def exchange(out_a, out_b):
    by_y = lax.all_to_all(out_a, "dp", 0, 0, axis_index_groups=Y_GROUPS, tiled=True)
    made = {"sums": sum_y(by_y)}

    def tie(k, up, down):
        if k == STIE:
            up, down, made["sums"] = lax.optimization_barrier((up, down, made["sums"]))
        return up, down

    own, *others = ring(out_b, tie)
    from_z = lax.all_to_all(made["sums"], "dp", 0, 0, axis_index_groups=Z_GROUPS, tiled=True)
    from_y = [own] + [lax.ppermute(x, "dp", shift(dy=d + 1)) for d, x in enumerate(others)]
    return from_z, from_y


def routing(edge_rows, edge_cols, edge_counts, block_owner, z, y, c):
    live = jnp.arange(EDGES // 2, dtype=jnp.int32) < edge_counts[0]
    code = jnp.where(live, block_owner[edge_cols], -1)
    mine = jnp.stack([code, edge_rows])
    theirs = lax.ppermute(mine, "dp", shift(dc=1))
    code = jnp.concatenate([mine[0], theirs[0]])
    rows = jnp.concatenate([mine[1], theirs[1] + NB])
    dev = code // NB
    used = (code >= 0) & (dev % NC == c)
    y_to, z_to = (dev // NC) % NY, dev // (NC * NY)
    slot = jnp.where(used, ((z_to - z + NZ) % NZ * NY + (y_to - y + NY) % NY) * NB + code % NB, SLOTS)
    ids = jnp.arange(EDGES, dtype=jnp.int32)
    key = jnp.where(used, slot + SLOTS * (ids // (EDGES // 2)), 2 * SLOTS)
    keys = jnp.arange(2 * SLOTS, dtype=jnp.int32)
    same = (key[:, None] == key[None, :]) & (ids[None, :] < ids[:, None])
    rank = jnp.sum(same.astype(jnp.int32), axis=1)
    hit = (key[:, None] == keys[None, :]).astype(jnp.int32)
    pairs = (jnp.sum(hit, axis=0) + 1) // 2
    base = jnp.sum(jnp.where(keys[None, :] < keys[:, None], pairs[None, :], 0), axis=1)
    item = jnp.where(used, jnp.sum(hit * base[None, :], axis=1) + rank // 2, -1)
    side = rank % 2
    place = jnp.arange(ITEMS, dtype=jnp.int32)
    at = [
        (place[:, None] == item[None, :]) & (side[None, :] == s) for s in range(2)
    ]

    def pick(mask, values, default):
        return jnp.sum(jnp.where(mask, values[None, :] - default, 0), axis=1) + default

    return jnp.concatenate(
        [
            pick(at[0], slot, SLOTS),
            pick(at[0], ids, 0),
            pick(at[1], ids, 0),
            pick(at[0], rows, 2 * NB),
            pick(at[1], rows, 2 * NB),
            jnp.stack([jnp.sum(pairs), z, y, jnp.sum(pairs[:SLOTS])]),
        ]
    ).astype(jnp.int32)


def on_device(
    cotangent, saved_inputs, weights, edge_values, edge_rows, edge_cols, edge_counts, block_owner
):
    scale = 1.0 / math.sqrt(saved_inputs.shape[1] * lax.axis_size("dp"))
    dp = lax.axis_index("dp")
    z, y, c = dp // (NY * NC), dp // NC % NY, dp % NC
    group = lax.axis_index("group")
    member = jnp.full((1,), group, jnp.int32)

    edges_sib = lax.ppermute(edge_values, "dp", shift(dc=1))
    table = routing(edge_rows, edge_cols, edge_counts, block_owner, z, y, c)
    grad, slopes = first_slopes(member, saved_inputs, weights, cotangent)
    factor = [factors(member, saved_inputs, weights, h) for h in range(HOPS - 1)]

    my_rows = [
        lax.dynamic_slice(weights, (h, group * BLK, 0), (1, BLK, 512))[0] for h in range(HOPS)
    ]
    sums = [None] * HOPS
    for hop in reversed(range(HOPS)):
        pieces = [slopes] + [
            lax.ppermute(slopes, "group", [(i, (i + d) % NX) for i in range(NX)])
            for d in range(1, NX)
        ]
        weight = weight_part(saved_inputs, slopes, hop, scale)
        pieces[-1], weight = lax.optimization_barrier((pieces[-1], weight))
        own = upstream_of(member, my_rows[hop], pieces)
        sibling = lax.ppermute(own, "dp", shift(dc=1))
        out_a, *out_b = messages_of(table, own, sibling, edge_values, edges_sib, weight)
        from_z, from_y = exchange(out_a, out_b)
        if hop:
            grad, slopes, sums[hop] = update(from_z, from_y, grad, factor[hop - 1])
    result = last_update(from_z, from_y, grad)
    sums[0] = last_sums(from_z)
    return result, collect(spread(jnp.concatenate(sums, axis=0)))


def solution(mesh):
    in_specs = (
        P("dp", "group"),
        P(None, "dp", None),
        P(),
        P("dp", None, None),
        P("dp"),
        P("dp"),
        P("dp"),
        P(),
    )
    out_specs = (P("dp", "group"), P(None, None, "group"))
    return jax.shard_map(
        on_device, mesh=mesh, in_specs=in_specs, out_specs=out_specs, check_vma=False
    )
```
